32 devices in a mesh: gx: 2 (over core), gy: 4 (over y, x), gz: 4 (over z).
Axes of the slice: x: 2, y: 2, z: 4, core: 2. Of those that a mesh axis runs over, the one named last changes fastest.
Arguments:
- displacement: float32 [3, 16, 64, 512], P(None, 'gx', 'gy', 'gz'), may hold values from -6 to 6
- adjoint_load: float32 [3, 16, 64, 512], P(None, 'gx', 'gy', 'gz'), may hold values from -6 to 6
- bone_mask: int32 [16, 64, 512], P('gx', 'gy', 'gz'), may hold values 0 or 1
- elem_zone: int32 [16, 64, 512], P('gx', 'gy', 'gz'), may hold values from 0 to 127, as said below
- zone_slot: int32 [128], replicated, may hold values from 0 to 127, each once
- zone_modulus: float32 [128], P(('gx', 'gy', 'gz')), may hold values from 0.5 to 4
Outputs:
- adjoint: float32 [3, 16, 64, 512], P(None, 'gx', 'gy', 'gz')
- zone_gradient: float32 [128], P(('gx', 'gy', 'gz'))
The draws below stay inside these ranges and needn't reach their ends.
Inputs may be any that keep to these rules, and one draw needn't show every extreme that they name: `elem_zone`: zones are cubes of 16 voxels on a grid shifted by a drawn offset that wraps cyclically, so a cube cut by one end of the window continues at the other end under the same number; zones are numbered in a drawn order and every zone number occurs. `zone_slot`: each zone appears at exactly one position.
All inputs are finite; a program needn't handle non-finite values. No bound on the sum of `bone_mask` on one device may be relied on, other than what follows from the above.
Results may differ from the reference program's by a relative error of at most 0.0003.
Values sent between devices are 32-bit elements; how exact they have to be, the bound alone decides.
A program may use at most 64 MiB of HBM per device.

```python
import math
import jax
import jax.numpy as jnp
import numpy as np
from jax import lax

CX = 8
ZS = 16
ITERS = 2
NX = 16
NY = 64
NZ = 512
ZONES = 128


def draw_elem_zone(key, part):
    offsets = jax.random.randint(jax.random.fold_in(key, 11), (3,), 0, ZS)
    labels = jax.random.permutation(jax.random.fold_in(key, 23), ZONES).astype(jnp.int32)
    zone_x = (lax.broadcasted_iota(jnp.int32, (NX, NY, NZ), 0) + offsets[0]) // ZS % (NX // ZS)
    zone_y = (lax.broadcasted_iota(jnp.int32, (NX, NY, NZ), 1) + offsets[1]) // ZS % (NY // ZS)
    zone_z = (lax.broadcasted_iota(jnp.int32, (NX, NY, NZ), 2) + offsets[2]) // ZS % (NZ // ZS)
    cell = (zone_x * (NY // ZS * (NZ // ZS)) + zone_y * (NZ // ZS) + zone_z).astype(jnp.int32)
    return jnp.take(labels, cell).astype(jnp.int32)


def place_ends(values, key, low, largest):
    spot = [jax.random.randint(jax.random.fold_in(key, axis), (), 0, length) for axis, length in enumerate(values.shape)]
    longest = values.shape.index(max(values.shape))
    beside = spot[:longest] + [(spot[longest] + 1) % values.shape[longest]] + spot[longest + 1:]
    return values.at[tuple(spot)].set(low).at[tuple(beside)].set(largest)


def levels(stream_key, shape, cuts, smallest, high):
    loudness, own = 1.0, jax.random.fold_in(stream_key, 6)
    for axis_at, shards_of in cuts:
        steps = jnp.exp(jax.random.uniform(jax.random.fold_in(own, axis_at), (shards_of,), jnp.float32, smallest / len(cuts), high / len(cuts)))
        loudness = loudness * jnp.repeat(steps, shape[axis_at] // shards_of).reshape([-1 if axis == axis_at else 1 for axis in range(len(shape))])
    return loudness


def scatter_about(stream_key, shape, width, bound, shards=(), kind=jnp.bfloat16):
    level = levels(stream_key, shape, shards, -0.22, 0.18) if shards else 1.0
    values = jax.random.normal(stream_key, shape, jnp.float32) * width * level
    return jnp.minimum(jnp.maximum(values, -bound), bound).astype(kind)


def setup_inputs(seed: int = 0) -> dict:
    splits = jax.random.split(jax.random.key(seed), 7)
    displacement = scatter_about(splits[0], (3, NX, NY, NZ), 1.0, 6.0, ((1, 2), (2, 4), (3, 4)), jnp.float32)
    adjoint_load = scatter_about(splits[1], (3, NX, NY, NZ), 1.0, 6.0, ((1, 2), (2, 4), (3, 4)), jnp.float32)
    bone_mask = place_ends((jax.random.randint(splits[2], (NX, NY, NZ), 0, 2) < 1).astype(jnp.int32), jax.random.fold_in(splits[2], 1), 0, 1)
    elem_zone = draw_elem_zone(jax.random.fold_in(splits[6], 71), 0)
    zone_slot = jax.random.permutation(splits[4], ZONES).astype(jnp.int32)
    zone_modulus = jnp.clip(jnp.exp(math.log(4.0) - 2.0794415 * jax.random.uniform(splits[5], (ZONES,), jnp.float32) ** levels(splits[5], (ZONES,), ((0, 32),), -0.2, 0.2)), 0.5, 4.0)
    return {"displacement": displacement, "adjoint_load": adjoint_load, "bone_mask": bone_mask, "elem_zone": elem_zone, "zone_slot": zone_slot, "zone_modulus": zone_modulus}


spring_rate = 0.1

def hex_stiffness():
    poisson = 0.3
    lame_first = poisson / ((1.0 + poisson) * (1.0 - 2.0 * poisson))
    shear_mod = 0.5 / (1.0 + poisson)
    elastic = np.zeros((6, 6))
    elastic[:3, :3] = lame_first
    for index in range(3):
        elastic[index, index] += 2.0 * shear_mod
        elastic[index + 3, index + 3] = shear_mod
    corner_signs = np.array([[2.0 * (corner // 4) - 1.0, 2.0 * (corner // 2 % 2) - 1.0, 2.0 * (corner % 2) - 1.0] for corner in range(8)])
    gauss_value = 1.0 / np.sqrt(3.0)
    stiffness = np.zeros((24, 24))
    for gauss_x in (-gauss_value, gauss_value):
        for gauss_y in (-gauss_value, gauss_value):
            for gauss_z in (-gauss_value, gauss_value):
                where_at = np.array([gauss_x, gauss_y, gauss_z])
                strain_map = np.zeros((6, 24))
                for corner in range(8):
                    factor = 1.0 + corner_signs[corner] * where_at
                    grad_x = corner_signs[corner, 0] * factor[1] * factor[2] / 4.0
                    grad_y = corner_signs[corner, 1] * factor[0] * factor[2] / 4.0
                    grad_z = corner_signs[corner, 2] * factor[0] * factor[1] / 4.0
                    column = 3 * corner
                    strain_map[0, column] = grad_x
                    strain_map[1, column + 1] = grad_y
                    strain_map[2, column + 2] = grad_z
                    strain_map[3, column] = grad_y
                    strain_map[3, column + 1] = grad_x
                    strain_map[4, column + 1] = grad_z
                    strain_map[4, column + 2] = grad_y
                    strain_map[5, column] = grad_z
                    strain_map[5, column + 2] = grad_x
                stiffness += strain_map.T @ elastic @ strain_map / 8.0
    return stiffness

def corner_stack(field_in):
    rows_x = field_in.shape[1] - 1
    rows_y = field_in.shape[2] - 1
    rows_z = field_in.shape[3] - 1
    pieces = []
    for corner in range(8):
        shift_x, shift_y, shift_z = (corner // 4, corner // 2 % 2, corner % 2)
        pieces.append(field_in[:, shift_x:shift_x + rows_x, shift_y:shift_y + rows_y, shift_z:shift_z + rows_z])
    return jnp.concatenate(pieces, axis=0)

def apply_local(field_in, moduli, stiffness):
    rows_x = field_in.shape[1] - 1
    rows_y = field_in.shape[2] - 1
    rows_z = field_in.shape[3] - 1
    stacked = corner_stack(field_in)
    forces = jnp.einsum('ij,jxyz->ixyz', stiffness, stacked, precision=lax.Precision.HIGHEST) * moduli[None]
    result = spring_rate * field_in[:, 1:-1, 1:-1, 1:-1]
    for corner in range(8):
        shift_x, shift_y, shift_z = (corner // 4, corner // 2 % 2, corner % 2)
        result = result + forces[3 * corner:3 * corner + 3, 1 - shift_x:1 - shift_x + rows_x - 1, 1 - shift_y:1 - shift_y + rows_y - 1, 1 - shift_z:1 - shift_z + rows_z - 1]
    return result

def element_terms(adjoint_nodes, disp_nodes, bone_float, stiffness):
    stacked_disp = corner_stack(disp_nodes)
    stacked_adj = corner_stack(adjoint_nodes)
    forces = jnp.einsum('ij,jxyz->ixyz', stiffness, stacked_disp, precision=lax.Precision.HIGHEST)
    return -ZS ** (-1.5) * lax.optimization_barrier(jnp.sum(stacked_adj * forces, axis=0)) * bone_float

def reference(displacement, adjoint_load, bone_mask, elem_zone, zone_slot, zone_modulus):
    stiffness = jnp.asarray(hex_stiffness(), dtype=jnp.float32)
    slot_map = jnp.take(zone_slot, elem_zone).astype(jnp.int32)
    bone_float = bone_mask.astype(jnp.float32)
    moduli = jnp.take(zone_modulus, slot_map) * bone_float
    moduli_pad = jnp.pad(moduli, ((1, 0), (1, 0), (1, 0)))
    slab_count = NX // CX
    slab_ids = jnp.arange(slab_count, dtype=jnp.int32)

    def operate(field_in):
        padded = jnp.pad(field_in, ((0, 0), (1, 1), (1, 1), (1, 1)))

        def one_slab(slab_index):
            offset = (slab_index * CX).astype(jnp.int32)
            piece = lax.dynamic_slice_in_dim(padded, offset, CX + 2, 1)
            mod_piece = lax.dynamic_slice_in_dim(moduli_pad, offset, CX + 1, 0)
            return apply_local(piece, mod_piece, stiffness)
        blocks = lax.map(one_slab, slab_ids)
        return jnp.transpose(blocks, (1, 0, 2, 3, 4)).reshape(3, NX, NY, NZ)
    adjoint = jnp.zeros_like(adjoint_load)
    residual = adjoint_load
    direction = adjoint_load
    norm_now = jnp.sum(residual * residual)
    for step_index in range(ITERS):
        applied = operate(direction)
        step_size = norm_now / jnp.sum(direction * applied)
        adjoint = adjoint + step_size * direction
        residual = residual - step_size * applied
        fresh = jnp.sum(residual * residual)
        direction = residual + fresh / norm_now * direction
        norm_now = fresh
    adj_pad = jnp.pad(adjoint, ((0, 0), (0, 1), (0, 1), (0, 1)))
    disp_pad = jnp.pad(displacement, ((0, 0), (0, 1), (0, 1), (0, 1)))

    def accumulate(carry, slab_index):
        offset = (slab_index * CX).astype(jnp.int32)
        adj_piece = lax.dynamic_slice_in_dim(adj_pad, offset, CX + 1, 1)
        disp_piece = lax.dynamic_slice_in_dim(disp_pad, offset, CX + 1, 1)
        bone_piece = lax.dynamic_slice_in_dim(bone_float, offset, CX, 0)
        slot_piece = lax.dynamic_slice_in_dim(slot_map, offset, CX, 0)
        terms = element_terms(adj_piece, disp_piece, bone_piece, stiffness)
        return (carry + jax.ops.segment_sum(terms.ravel(), slot_piece.ravel(), num_segments=ZONES), None)
    zone_gradient, unused = lax.scan(accumulate, jnp.zeros((ZONES,), jnp.float32), slab_ids)
    return (adjoint, zone_gradient)
```

```python
import functools
import jax
import jax.numpy as jnp
from jax import lax
from jax.experimental import pallas as pl
from jax.experimental.pallas import tpu as pltpu
from jax.sharding import PartitionSpec as P

ZS = 16
SPRING = 0.1
MESH = pl.DeviceIdType.MESH
LAME = 0.3 / (1.3 * 0.4)
SHEAR = 0.5 / 1.3
F32 = jnp.float32
LOW = 5


def element_forces(m):
    c = 1.0 / 16.0
    lam, mu = c * LAME, c * SHEAR
    lam3, mu3 = lam / 3.0, mu / 3.0
    u, v, w = m
    f = [[[[None, None], [None, None]], [[None, None], [None, None]]] for _ in range(3)]
    div = lam * (u[1][0][0] + v[0][1][0] + w[0][0][1])
    f[0][1][0][0] = div + (2 * mu) * u[1][0][0]
    f[1][0][1][0] = div + (2 * mu) * v[0][1][0]
    f[2][0][0][1] = div + (2 * mu) * w[0][0][1]
    f[0][0][1][0] = f[1][1][0][0] = mu * (u[0][1][0] + v[1][0][0])
    f[1][0][0][1] = f[2][0][1][0] = mu * (v[0][0][1] + w[0][1][0])
    f[0][0][0][1] = f[2][1][0][0] = mu * (u[0][0][1] + w[1][0][0])
    t = lam3 * (u[1][1][0] + w[0][1][1])
    f[0][1][1][0] = t + mu * u[1][1][0]
    f[2][0][1][1] = t + mu * w[0][1][1]
    t = lam3 * (u[1][0][1] + v[0][1][1])
    f[0][1][0][1] = t + mu * u[1][0][1]
    f[1][0][1][1] = t + mu * v[0][1][1]
    t = lam3 * (v[1][1][0] + w[1][0][1])
    f[1][1][1][0] = t + mu * v[1][1][0]
    f[2][1][0][1] = t + mu * w[1][0][1]
    t = u[0][1][1] + v[1][0][1] + w[1][1][0]
    f[0][0][1][1] = mu3 * (t + u[0][1][1])
    f[1][1][0][1] = mu3 * (t + v[1][0][1])
    f[2][1][1][0] = mu3 * (t + w[1][1][0])
    for k in range(3):
        f[k][1][1][1] = ((lam + 4 * mu) / 9.0) * m[k][1][1][1]
    return f


def modes_of(load, x):
    out = []
    for k in range(3):
        here = [[load(4 * k + 2 * b + c, x) for c in range(2)] for b in range(2)]
        there = [[load(4 * k + 2 * b + c, x + 1) for c in range(2)] for b in range(2)]
        out.append([
            [[None if b + c == 0 else there[b][c] + here[b][c] for c in range(2)] for b in range(2)],
            [[there[b][c] - here[b][c] for c in range(2)] for b in range(2)],
        ])
    return out


ALL = [(k, a, b, c) for k in range(3) for a in range(2) for b in range(2) for c in range(2) if a + b + c]


def dot_modes(f, g):
    total = None
    for k, a, b, c in ALL:
        t = f[k][a][b][c] * g[k][a][b][c]
        total = t if total is None else total + t
    return total


def kernel(sizes, disp, load, mask, zone, slot_ref, mod_ref, adj_ref, grad_ref,
           E, BM, DM, NB, Q, QM, TB, G, MS, R, ZPL, ZPH, ZL, ZH, YPL, YPH, YL, YH,
           ag_send, ag_recv, rs_send, rs_recv, hs, hr):
    nx, ny, nz = sizes
    n = nx * ny * nz
    cx, cy, cz = mask.shape
    wy, wz = cy + 8, 2 * cz
    per = mod_ref.shape[0]
    rows = slot_ref.shape[0]
    ix, iy, iz = lax.axis_index("gx"), lax.axis_index("gy"), lax.axis_index("gz")
    me = (ix * ny + iy) * nz + iz

    def place(t):
        return (t // (ny * nz), (t // nz) % ny, t % nz)

    lane1 = lax.broadcasted_iota(jnp.int32, (1, 128), 1)
    row = jnp.zeros((1, 128), F32)
    for j in range(per):
        row = jnp.where(lane1 == (me * per) % 128 + j, mod_ref[j], row)
    G[me] = row

    def send_mod(o, carry):
        t = (me + o) % n
        pltpu.make_async_remote_copy(
            src_ref=G.at[me], dst_ref=G.at[me], send_sem=ag_send, recv_sem=ag_recv,
            device_id=place(t), device_id_type=MESH).start()
        return carry
    lax.fori_loop(1, n, send_mod, 0)

    def exchange(axis, spot, count, low_src, high_dst, high_src, low_dst, s):
        down = pltpu.make_async_remote_copy(
            src_ref=low_src, dst_ref=high_dst, send_sem=hs.at[s], recv_sem=hr.at[s],
            device_id={axis: jnp.maximum(spot - 1, 0)}, device_id_type=MESH)
        up = pltpu.make_async_remote_copy(
            src_ref=high_src, dst_ref=low_dst, send_sem=hs.at[s + 1], recv_sem=hr.at[s + 1],
            device_id={axis: jnp.minimum(spot + 1, count - 1)}, device_id_type=MESH)

        @pl.when(spot > 0)
        def _():
            down.start()

        @pl.when(spot < count - 1)
        def _():
            up.start()

        @pl.when(spot == 0)
        def _():
            low_dst[...] = jnp.zeros(low_dst.shape, F32)

        @pl.when(spot == count - 1)
        def _():
            high_dst[...] = jnp.zeros(high_dst.shape, F32)

        @pl.when(spot > 0)
        def _():
            down.wait_send()
            up.wait_recv()

        @pl.when(spot < count - 1)
        def _():
            up.wait_send()
            down.wait_recv()

    lane = lax.broadcasted_iota(jnp.int32, (cy, 128), 1)

    def fill(x, carry):
        low, high = carry
        for f in range(8):
            if f < 3:
                value = load[f, x]
            elif f == 3:
                value = mask[x].astype(F32)
            elif f == 4:
                value = zone[x].astype(F32)
            else:
                value = disp[f - 5, x]
            E[f, x + 1, 0:cy, 0:cz] = value
            low = jnp.where(lane == f * 8 + x, pltpu.roll(value, f * 8 + x, 1), low)
            if f < 3:
                low = jnp.where(lane == (8 + f) * 8 + x, pltpu.roll(value, (8 + f) * 8 + x - 1, 1), low)
            if f < LOW:
                high = jnp.where(lane == f * 8 + x, pltpu.roll(value, f * 8 + x + 1, 1), high)
        return low, high
    zero = jnp.zeros((cy, 128), F32)
    low, high = lax.fori_loop(0, cx, fill, (zero, zero))
    ZPL[...] = low
    ZPH[...] = high
    exchange("gz", iz, nz, ZPL, ZH, ZPH, ZL, 0)

    def open_z(x, carry):
        above, below = ZH[...], ZL[...]
        for f in range(8):
            tile = jnp.where(lane == 0, pltpu.roll(above, 128 - f * 8 - x, 1), 0.0)
            if f < 3:
                tile = jnp.where(lane == 1, pltpu.roll(above, 128 + 1 - (8 + f) * 8 - x, 1), tile)
            if f < LOW:
                tile = jnp.where(lane == 127, pltpu.roll(below, 127 - f * 8 - x, 1), tile)
            E[f, x + 1, 0:cy, cz:wz] = tile
        return carry
    lax.fori_loop(0, cx, open_z, 0)

    for f in range(8):
        YPL[f] = E[f, 1:cx + 1, 0, :]
        if f < 3:
            YPL[8 + f] = E[f, 1:cx + 1, 1, :]
        if f < LOW:
            YPH[f] = E[f, 1:cx + 1, cy - 1, :]
    exchange("gy", iy, ny, YPL, YH, YPH, YL, 2)
    line = lax.broadcasted_iota(jnp.int32, (8, wz), 0)
    for f in range(8):
        above = YH[f]
        second = YH[8 + f] if f < 3 else None
        below = YL[f] if f < LOW else None
        for x in range(cx):
            tile = jnp.where(line == 0, above[x:x + 1], 0.0)
            if f < 3:
                tile = jnp.where(line == 1, second[x:x + 1], tile)
            if f < LOW:
                tile = jnp.where(line == 7, below[x:x + 1], tile)
            E[f, x + 1, cy:wy, :] = tile
    exchange("gx", ix, nx, E.at[:, pl.ds(1, 2)], E.at[:, pl.ds(cx + 1, 2)],
             E.at[pl.ds(0, LOW), pl.ds(cx, 1)], E.at[pl.ds(0, LOW), pl.ds(0, 1)], 4)

    whole = G.at[pl.ds(0, n - 1)]
    pltpu.make_async_copy(whole, whole, ag_recv).wait()
    pltpu.make_async_copy(whole, whole, ag_send).wait()
    group = n // rows
    by_slot = [jnp.sum(G[g * group:(g + 1) * group, 0, :], axis=0, keepdims=True) for g in range(rows)]

    def look_up(tables, index):
        tables = [jnp.broadcast_to(t, (8, 128)) for t in tables]
        low_bits, which = index % 128, index // 128
        out = None
        for g, t in enumerate(tables):
            got = jnp.take_along_axis(t, low_bits, axis=1, mode="promise_in_bounds")
            out = got if out is None else jnp.where(which == g, got, out)
        return out
    by_zone = []
    for g in range(rows):
        index = jnp.broadcast_to(slot_ref[g:g + 1, :], (8, 128))
        by_zone.append(look_up(by_slot, index)[0:1])

    def yz_modes(v, put, x, k):
        after = pltpu.roll(v, wz - 1, 1)
        for c, t in enumerate((v + after, after - v)):
            above = pltpu.roll(t, wy - 1, 0)
            put(4 * k + c, x, t + above)
            put(4 * k + 2 + c, x, above - t)

    def put_b(i, x, v):
        BM[i, x] = v

    def put_d(i, x, v):
        DM[i, x] = v[0:cy, 0:cz]

    def put_q(i, x, v):
        QM[i, x] = v[0:cy, 0:cz]

    def b_modes(x, carry):
        for k in range(3):
            yz_modes(E[k, x], put_b, x, k)
        return carry
    lax.fori_loop(0, cx + 3, b_modes, 0)

    def d_modes(x, carry):
        for k in range(3):
            yz_modes(E[5 + k, x + 1], put_d, x, k)
        return carry
    lax.fori_loop(0, cx + 1, d_modes, 0)

    def first(x, carry):
        where = E[4, x].astype(jnp.int32)
        parts = []
        for y in range(0, wy, 8):
            parts.append(jnp.concatenate(
                [look_up(by_zone, where[y:y + 8, z:z + 128]) for z in range(0, wz, 128)], axis=1))
        stiff = jnp.where(E[3, x] > 0.5, jnp.concatenate(parts, axis=0), 0.0)
        TB[1, x] = stiff[0:cy, 0:cz]
        f = element_forces(modes_of(lambda i, p: BM[i, p], x))

        @pl.when(jnp.logical_and(x > 0, x <= cx))
        def _():
            inner = [[[[None if t is None else t[0:cy, 0:cz] for t in b] for b in a] for a in k] for k in f]
            TB[0, x] = dot_modes(inner, modes_of(lambda i, p: DM[i, p], x - 1))
        for k in range(3):
            for b in range(2):
                for c in range(2):
                    i = 4 * k + 2 * b + c
                    delta = f[k][1][b][c] * stiff
                    if b + c:
                        total = f[k][0][b][c] * stiff
                        now, later = total - delta, total + delta
                    else:
                        now, later = -delta, delta
                    NB[i, x] = NB[i, x] + now
                    NB[i, x + 1] = later
        return carry
    for i in range(12):
        NB[i, 0] = jnp.zeros((wy, wz), F32)
    lax.fori_loop(0, cx + 2, first, 0)

    at_y = lax.broadcasted_iota(jnp.int32, (wy, wz), 0)
    at_z = lax.broadcasted_iota(jnp.int32, (wy, wz), 1)
    last_x, last_y, last_z = ix == nx - 1, iy == ny - 1, iz == nz - 1
    keep_y = jnp.where(last_y, cy, wy)
    keep_z = jnp.where(last_z, cz, wz)
    inside = jnp.logical_and(at_y < keep_y, at_z < keep_z)

    def nodes(x, carry):
        bq, qq, bb = carry
        keep_x = jnp.where(last_x, cx, cx + 1)
        valid = jnp.logical_and(inside, jnp.broadcast_to(x, (wy, wz)) < keep_x)
        own = jnp.where(x < cx, 1.0, 0.0).astype(F32)
        for k in range(3):
            side = []
            for c in range(2):
                s, d = NB[4 * k + c, x + 1], NB[4 * k + 2 + c, x + 1]
                side.append((s - d) + pltpu.roll(s + d, 1, 0))
            q = (side[0] - side[1]) + pltpu.roll(side[0] + side[1], 1, 1)
            q = jnp.where(valid, q, 0.0)
            mine = q[0:cy, 0:cz]
            Q[k, x] = mine
            v = E[k, x + 1, 0:cy, 0:cz]
            bq = bq + own * (v * mine)
            qq = qq + own * (mine * mine)
            bb = bb + own * (v * v)
            yz_modes(q, put_q, x, k)
        return bq, qq, bb
    bq, qq, bb = lax.fori_loop(0, cx + 1, nodes, (zero, zero, zero))

    scale = -(ZS ** -1.5)
    first_zone = zone[0]

    def second(x, carry):
        energy, a1, a2, b1, b2 = carry
        m = modes_of(lambda i, p: QM[i, p], x)
        f = element_forces(m)
        energy = energy + TB[1, x + 1] * dot_modes(f, m)
        bone = scale * mask[x].astype(F32)
        t2 = bone * dot_modes(f, modes_of(lambda i, p: DM[i, p], x))
        t1 = bone * TB[0, x + 1]
        same = zone[x] == first_zone
        a1 = a1 + jnp.where(same, t1, 0.0)
        a2 = a2 + jnp.where(same, t2, 0.0)
        b1 = b1 + jnp.where(same, 0.0, t1)
        b2 = b2 + jnp.where(same, 0.0, t2)
        return energy, a1, a2, b1, b2
    energy, a1, a2, b1, b2 = lax.fori_loop(0, cx, second, (zero,) * 5)

    owner = lax.broadcasted_iota(jnp.int32, (n, 128), 0)
    sub = lax.broadcasted_iota(jnp.int32, (16, 128), 0)
    slots = [slot_ref[g:g + 1, :] for g in range(rows)]
    out = jnp.zeros((n, 16), F32)
    for zones, t1, t2 in ((first_zone, a1, a2), (zone[cx - 1], b1, b2)):
        same = zones == zones[0:1]
        for at, cond in ((0, same), (cy - 1, jnp.logical_not(same))):
            v1 = jnp.sum(jnp.where(cond, t1, 0.0), axis=0, keepdims=True)
            v2 = jnp.sum(jnp.where(cond, t2, 0.0), axis=0, keepdims=True)
            k = look_up(slots, jnp.broadcast_to(zones[at:at + 1], (8, 128)))[0:1]
            own_by, part = k // per, k % per
            w = jnp.where(owner == own_by, 1.0, 0.0).astype(F32)
            v = jnp.where(sub == part, v1, jnp.where(sub == part + per, v2, 0.0))
            out = out + lax.dot_general(w, v, (((1,), (1,)), ((), ())),
                                        precision=lax.Precision.HIGHEST, preferred_element_type=F32)
    lane16 = lax.broadcasted_iota(jnp.int32, (n, 16), 1)
    for j, value in enumerate((bb, bq, qq, energy)):
        value = jnp.sum(jnp.sum(value, axis=0, keepdims=True), axis=1, keepdims=True)
        out = jnp.where(lane16 == 2 * per + j, value, out)
    MS[...] = jnp.zeros_like(MS)
    MS[:, 0, 0:16] = out

    def send_sum(o, carry):
        t = (me + o) % n
        pltpu.make_async_remote_copy(
            src_ref=MS.at[t], dst_ref=R.at[n - 1 - o], send_sem=rs_send, recv_sem=rs_recv,
            device_id=place(t), device_id_type=MESH).start()
        return carry
    lax.fori_loop(1, n, send_sum, 0)
    pltpu.make_async_copy(R, R, rs_recv).wait()
    pltpu.make_async_copy(R, R, rs_send).wait()
    row = jnp.sum(R[:, 0, :], axis=0, keepdims=True) + MS[me]

    def pick(j):
        return jnp.sum(jnp.where(lane1 == 2 * per + j, row, 0.0), axis=1, keepdims=True)
    bb, bq, qq, qkq = pick(0), pick(1), pick(2), pick(3)
    gram = bb * qq - bq * bq
    top = SPRING * gram + (bb * qkq - bq * qq)
    det = SPRING * top + (bq * qkq - qq * qq)
    plane = det != 0.0
    c1 = jnp.where(plane, top / det, bb / (SPRING * bb + bq))
    c2 = jnp.where(plane, -gram / det, 0.0)
    both = c1 * row + c2 * pltpu.roll(row, 128 - per, 1)
    grad_ref[...] = both[:, 0:per]

    def finish(x, carry):
        for k in range(3):
            adj_ref[k, x] = c1 * load[k, x] + c2 * Q[k, x]
        return carry
    lax.fori_loop(0, cx, finish, 0)


def solution(mesh):
    sizes = (mesh.shape["gx"], mesh.shape["gy"], mesh.shape["gz"])
    n = sizes[0] * sizes[1] * sizes[2]

    def on_device(displacement, adjoint_load, bone_mask, elem_zone, zone_slot, zone_modulus):
        cx, cy, cz = bone_mask.shape
        per = zone_modulus.shape[0]
        wy, wz = cy + 8, 2 * cz
        vm = pl.BlockSpec(memory_space=pltpu.VMEM)
        scratch = [
            (8, cx + 3, wy, wz), (12, cx + 3, wy, wz), (12, cx + 1, cy, cz), (12, cx + 3, wy, wz),
            (3, cx + 1, cy, cz), (12, cx + 1, cy, cz), (2, cx + 2, cy, cz),
            (n, 1, 128), (n, 1, 128), (n - 1, 1, 128),
            (cy, 128), (cy, 128), (cy, 128), (cy, 128),
            (11, cx, wz), (LOW, cx, wz), (LOW, cx, wz), (11, cx, wz),
        ]
        adjoint, gradient = pl.pallas_call(
            functools.partial(kernel, sizes),
            out_shape=(jax.ShapeDtypeStruct(adjoint_load.shape, F32), jax.ShapeDtypeStruct((1, per), F32)),
            in_specs=[vm] * 5 + [pl.BlockSpec(memory_space=pltpu.SMEM)],
            out_specs=(vm, vm),
            scratch_shapes=[pltpu.VMEM(s, F32) for s in scratch]
            + [pltpu.SemaphoreType.DMA] * 4 + [pltpu.SemaphoreType.DMA((6,))] * 2,
            compiler_params=pltpu.CompilerParams(has_side_effects=True, vmem_limit_bytes=40 * 2**20),
            cost_estimate=pl.CostEstimate(flops=10**7, bytes_accessed=10**6, transcendentals=0),
        )(displacement, adjoint_load, bone_mask, elem_zone, zone_slot.reshape(-1, 128), zone_modulus)
        return adjoint, gradient.reshape(per)

    whole = P(None, "gx", "gy", "gz")
    brick = P("gx", "gy", "gz")
    owned = P(("gx", "gy", "gz"))
    return jax.shard_map(on_device, mesh=mesh, in_specs=(whole, whole, brick, brick, P(), owned),
                         out_specs=(whole, owned), check_vma=False)
```

```python
import functools
import jax
import jax.numpy as jnp
from jax import lax
from jax.experimental import pallas as pl
from jax.experimental.pallas import tpu as pltpu
from jax.sharding import PartitionSpec as P

ZS = 16
SPRING = 0.1
MESH = pl.DeviceIdType.MESH
LAME = 0.3 / (1.3 * 0.4)
SHEAR = 0.5 / 1.3
F32 = jnp.float32
LOW = 5


def element_forces(m):
    c = 1.0 / 16.0
    lam, mu = c * LAME, c * SHEAR
    lam3, mu3 = lam / 3.0, mu / 3.0
    u, v, w = m
    f = [[[[None, None], [None, None]], [[None, None], [None, None]]] for _ in range(3)]
    div = lam * (u[1][0][0] + v[0][1][0] + w[0][0][1])
    f[0][1][0][0] = div + (2 * mu) * u[1][0][0]
    f[1][0][1][0] = div + (2 * mu) * v[0][1][0]
    f[2][0][0][1] = div + (2 * mu) * w[0][0][1]
    f[0][0][1][0] = f[1][1][0][0] = mu * (u[0][1][0] + v[1][0][0])
    f[1][0][0][1] = f[2][0][1][0] = mu * (v[0][0][1] + w[0][1][0])
    f[0][0][0][1] = f[2][1][0][0] = mu * (u[0][0][1] + w[1][0][0])
    t = lam3 * (u[1][1][0] + w[0][1][1])
    f[0][1][1][0] = t + mu * u[1][1][0]
    f[2][0][1][1] = t + mu * w[0][1][1]
    t = lam3 * (u[1][0][1] + v[0][1][1])
    f[0][1][0][1] = t + mu * u[1][0][1]
    f[1][0][1][1] = t + mu * v[0][1][1]
    t = lam3 * (v[1][1][0] + w[1][0][1])
    f[1][1][1][0] = t + mu * v[1][1][0]
    f[2][1][0][1] = t + mu * w[1][0][1]
    t = u[0][1][1] + v[1][0][1] + w[1][1][0]
    f[0][0][1][1] = mu3 * (t + u[0][1][1])
    f[1][1][0][1] = mu3 * (t + v[1][0][1])
    f[2][1][1][0] = mu3 * (t + w[1][1][0])
    for k in range(3):
        f[k][1][1][1] = ((lam + 4 * mu) / 9.0) * m[k][1][1][1]
    return f


def modes_of(load, x):
    out = []
    for k in range(3):
        here = [[load(4 * k + 2 * b + c, x) for c in range(2)] for b in range(2)]
        there = [[load(4 * k + 2 * b + c, x + 1) for c in range(2)] for b in range(2)]
        out.append([
            [[None if b + c == 0 else there[b][c] + here[b][c] for c in range(2)] for b in range(2)],
            [[there[b][c] - here[b][c] for c in range(2)] for b in range(2)],
        ])
    return out


ALL = [(k, a, b, c) for k in range(3) for a in range(2) for b in range(2) for c in range(2) if a + b + c]


def dot_modes(f, g):
    total = None
    for k, a, b, c in ALL:
        t = f[k][a][b][c] * g[k][a][b][c]
        total = t if total is None else total + t
    return total


def kernel(sizes, disp_in, load_in, mask_in, zone_in, slot_in, mod_in, adj_ref, grad_ref,
           disp, load, mask, zone, slot_ref, mod_ref,
           E, BM, DM, NB, Q, QM, TB, G, MS, R, ZPL, ZPH, ZL, ZH, YPL, YPH, YL, YH,
           ag_send, ag_recv, rs_send, rs_recv, hs, hr, ins):
    nx, ny, nz = sizes
    n = nx * ny * nz
    cx, cy, cz = mask.shape
    wy, wz = cy + 8, 2 * cz
    per = mod_ref.shape[0]
    rows = slot_ref.shape[0]
    ix, iy, iz = lax.axis_index("gx"), lax.axis_index("gy"), lax.axis_index("gz")
    me = (ix * ny + iy) * nz + iz

    barrier = pltpu.get_barrier_semaphore()
    offsets = [(a, b, c) for a in range(nx) for b in range(ny) for c in range(nz)][1:]

    def around(spot, step, count):
        if step == 0:
            return spot
        there = spot + step
        return jnp.where(there >= count, there - count, there)
    xs = [around(ix, a, nx) for a in range(nx)]
    ys = [around(iy, b, ny) for b in range(ny)]
    zs = [around(iz, c, nz) for c in range(nz)]

    def slot_at(a, b, c):
        return ((-a % nx) * ny + (-b % ny)) * nz + (-c % nz) - 1

    for a, b, c in offsets:
        pl.semaphore_signal(barrier, inc=1, device_id=(xs[a], ys[b], zs[c]), device_id_type=MESH)
    copies = [pltpu.make_async_copy(src, dst, ins.at[i]) for i, (src, dst) in enumerate(
        ((mod_in, mod_ref), (load_in, load), (mask_in, mask), (zone_in, zone), (disp_in, disp),
         (slot_in, slot_ref)))]
    for copy in copies:
        copy.start()
    for copy in copies:
        copy.wait()

    lane1 = lax.broadcasted_iota(jnp.int32, (1, 128), 1)
    row = jnp.zeros((1, 128), F32)
    for j in range(per):
        row = jnp.where(lane1 == (me * per) % 128 + j, mod_ref[j], row)
    G[me] = row

    def exchange(axis, spot, count, low_src, high_dst, high_src, low_dst, s):
        down = pltpu.make_async_remote_copy(
            src_ref=low_src, dst_ref=high_dst, send_sem=hs.at[s], recv_sem=hr.at[s],
            device_id={axis: jnp.maximum(spot - 1, 0)}, device_id_type=MESH)
        up = pltpu.make_async_remote_copy(
            src_ref=high_src, dst_ref=low_dst, send_sem=hs.at[s + 1], recv_sem=hr.at[s + 1],
            device_id={axis: jnp.minimum(spot + 1, count - 1)}, device_id_type=MESH)

        @pl.when(spot > 0)
        def _():
            down.start()

        @pl.when(spot < count - 1)
        def _():
            up.start()

        @pl.when(spot == 0)
        def _():
            low_dst[...] = jnp.zeros(low_dst.shape, F32)

        @pl.when(spot == count - 1)
        def _():
            high_dst[...] = jnp.zeros(high_dst.shape, F32)

        @pl.when(spot > 0)
        def _():
            down.wait_send()
            up.wait_recv()

        @pl.when(spot < count - 1)
        def _():
            up.wait_send()
            down.wait_recv()

    lane = lax.broadcasted_iota(jnp.int32, (cy, 128), 1)

    def fill(x, carry):
        low, high = carry
        for f in range(8):
            if f < 3:
                value = load[f, x]
            elif f == 3:
                value = mask[x].astype(F32)
            elif f == 4:
                value = zone[x].astype(F32)
            else:
                value = disp[f - 5, x]
            E[f, x + 1, 0:cy, 0:cz] = value
            low = jnp.where(lane == f * 8 + x, pltpu.roll(value, f * 8 + x, 1), low)
            if f < 3:
                low = jnp.where(lane == (8 + f) * 8 + x, pltpu.roll(value, (8 + f) * 8 + x - 1, 1), low)
            if f < LOW:
                high = jnp.where(lane == f * 8 + x, pltpu.roll(value, f * 8 + x + 1, 1), high)
        return low, high
    zero = jnp.zeros((cy, 128), F32)
    low, high = lax.fori_loop(0, cx, fill, (zero, zero))
    ZPL[...] = low
    ZPH[...] = high
    pl.semaphore_wait(barrier, n - 1)
    for a, b, c in offsets:
        pltpu.make_async_remote_copy(
            src_ref=G.at[me], dst_ref=G.at[me], send_sem=ag_send, recv_sem=ag_recv,
            device_id=(xs[a], ys[b], zs[c]), device_id_type=MESH).start()
    exchange("gz", iz, nz, ZPL, ZH, ZPH, ZL, 0)

    def open_z(x, carry):
        above, below = ZH[...], ZL[...]
        for f in range(8):
            tile = jnp.where(lane == 0, pltpu.roll(above, 128 - f * 8 - x, 1), 0.0)
            if f < 3:
                tile = jnp.where(lane == 1, pltpu.roll(above, 128 + 1 - (8 + f) * 8 - x, 1), tile)
            if f < LOW:
                tile = jnp.where(lane == 127, pltpu.roll(below, 127 - f * 8 - x, 1), tile)
            E[f, x + 1, 0:cy, cz:wz] = tile
        return carry
    lax.fori_loop(0, cx, open_z, 0)

    for f in range(8):
        YPL[f] = E[f, 1:cx + 1, 0, :]
        if f < 3:
            YPL[8 + f] = E[f, 1:cx + 1, 1, :]
        if f < LOW:
            YPH[f] = E[f, 1:cx + 1, cy - 1, :]
    exchange("gy", iy, ny, YPL, YH, YPH, YL, 2)
    line = lax.broadcasted_iota(jnp.int32, (8, wz), 0)
    for f in range(8):
        above = YH[f]
        second = YH[8 + f] if f < 3 else None
        below = YL[f] if f < LOW else None
        for x in range(cx):
            tile = jnp.where(line == 0, above[x:x + 1], 0.0)
            if f < 3:
                tile = jnp.where(line == 1, second[x:x + 1], tile)
            if f < LOW:
                tile = jnp.where(line == 7, below[x:x + 1], tile)
            E[f, x + 1, cy:wy, :] = tile
    exchange("gx", ix, nx, E.at[:, pl.ds(1, 2)], E.at[:, pl.ds(cx + 1, 2)],
             E.at[pl.ds(0, LOW), pl.ds(cx, 1)], E.at[pl.ds(0, LOW), pl.ds(0, 1)], 4)

    whole = G.at[pl.ds(0, n - 1)]
    pltpu.make_async_copy(whole, whole, ag_recv).wait()
    pltpu.make_async_copy(whole, whole, ag_send).wait()
    group = n // rows
    by_slot = [jnp.sum(G[g * group:(g + 1) * group, 0, :], axis=0, keepdims=True) for g in range(rows)]

    def look_up(tables, index):
        tables = [jnp.broadcast_to(t, (8, 128)) for t in tables]
        low_bits, which = index % 128, index // 128
        out = None
        for g, t in enumerate(tables):
            got = jnp.take_along_axis(t, low_bits, axis=1, mode="promise_in_bounds")
            out = got if out is None else jnp.where(which == g, got, out)
        return out
    by_zone = []
    for g in range(rows):
        index = jnp.broadcast_to(slot_ref[g:g + 1, :], (8, 128))
        by_zone.append(look_up(by_slot, index)[0:1])

    def yz_modes(v, put, x, k):
        after = pltpu.roll(v, wz - 1, 1)
        for c, t in enumerate((v + after, after - v)):
            above = pltpu.roll(t, wy - 1, 0)
            put(4 * k + c, x, t + above)
            put(4 * k + 2 + c, x, above - t)

    def put_b(i, x, v):
        BM[i, x] = v

    def put_d(i, x, v):
        DM[i, x] = v[0:cy, 0:cz]

    def put_q(i, x, v):
        QM[i, x] = v[0:cy, 0:cz]

    def b_modes(x, carry):
        for k in range(3):
            yz_modes(E[k, x], put_b, x, k)
        return carry
    lax.fori_loop(0, cx + 3, b_modes, 0)

    def d_modes(x, carry):
        for k in range(3):
            yz_modes(E[5 + k, x + 1], put_d, x, k)
        return carry
    lax.fori_loop(0, cx + 1, d_modes, 0)

    def first(x, carry):
        where = E[4, x].astype(jnp.int32)
        parts = []
        for y in range(0, wy, 8):
            parts.append(jnp.concatenate(
                [look_up(by_zone, where[y:y + 8, z:z + 128]) for z in range(0, wz, 128)], axis=1))
        stiff = jnp.where(E[3, x] > 0.5, jnp.concatenate(parts, axis=0), 0.0)
        TB[1, x] = stiff[0:cy, 0:cz]
        f = element_forces(modes_of(lambda i, p: BM[i, p], x))

        @pl.when(jnp.logical_and(x > 0, x <= cx))
        def _():
            inner = [[[[None if t is None else t[0:cy, 0:cz] for t in b] for b in a] for a in k] for k in f]
            TB[0, x] = dot_modes(inner, modes_of(lambda i, p: DM[i, p], x - 1))
        for k in range(3):
            for b in range(2):
                for c in range(2):
                    i = 4 * k + 2 * b + c
                    delta = f[k][1][b][c] * stiff
                    if b + c:
                        total = f[k][0][b][c] * stiff
                        now, later = total - delta, total + delta
                    else:
                        now, later = -delta, delta
                    NB[i, x] = NB[i, x] + now
                    NB[i, x + 1] = later
        return carry
    for i in range(12):
        NB[i, 0] = jnp.zeros((wy, wz), F32)
    lax.fori_loop(0, cx + 2, first, 0)

    at_y = lax.broadcasted_iota(jnp.int32, (wy, wz), 0)
    at_z = lax.broadcasted_iota(jnp.int32, (wy, wz), 1)
    last_x, last_y, last_z = ix == nx - 1, iy == ny - 1, iz == nz - 1
    keep_y = jnp.where(last_y, cy, wy)
    keep_z = jnp.where(last_z, cz, wz)
    inside = jnp.logical_and(at_y < keep_y, at_z < keep_z)

    def nodes(x, carry):
        bq, qq, bb = carry
        keep_x = jnp.where(last_x, cx, cx + 1)
        valid = jnp.logical_and(inside, jnp.broadcast_to(x, (wy, wz)) < keep_x)
        own = jnp.where(x < cx, 1.0, 0.0).astype(F32)
        for k in range(3):
            side = []
            for c in range(2):
                s, d = NB[4 * k + c, x + 1], NB[4 * k + 2 + c, x + 1]
                side.append((s - d) + pltpu.roll(s + d, 1, 0))
            q = (side[0] - side[1]) + pltpu.roll(side[0] + side[1], 1, 1)
            q = jnp.where(valid, q, 0.0)
            mine = q[0:cy, 0:cz]
            Q[k, x] = mine
            v = E[k, x + 1, 0:cy, 0:cz]
            bq = bq + own * (v * mine)
            qq = qq + own * (mine * mine)
            bb = bb + own * (v * v)
            yz_modes(q, put_q, x, k)
        return bq, qq, bb
    bq, qq, bb = lax.fori_loop(0, cx + 1, nodes, (zero, zero, zero))

    scale = -(ZS ** -1.5)
    first_zone = zone[0]

    def second(x, carry):
        energy, a1, a2, b1, b2 = carry
        m = modes_of(lambda i, p: QM[i, p], x)
        f = element_forces(m)
        energy = energy + TB[1, x + 1] * dot_modes(f, m)
        bone = scale * mask[x].astype(F32)
        t2 = bone * dot_modes(f, modes_of(lambda i, p: DM[i, p], x))
        t1 = bone * TB[0, x + 1]
        same = zone[x] == first_zone
        a1 = a1 + jnp.where(same, t1, 0.0)
        a2 = a2 + jnp.where(same, t2, 0.0)
        b1 = b1 + jnp.where(same, 0.0, t1)
        b2 = b2 + jnp.where(same, 0.0, t2)
        return energy, a1, a2, b1, b2
    energy, a1, a2, b1, b2 = lax.fori_loop(0, cx, second, (zero,) * 5)

    owner = lax.broadcasted_iota(jnp.int32, (n, 128), 0)
    sub = lax.broadcasted_iota(jnp.int32, (16, 128), 0)
    slots = [slot_ref[g:g + 1, :] for g in range(rows)]
    out = jnp.zeros((n, 16), F32)
    for zones, t1, t2 in ((first_zone, a1, a2), (zone[cx - 1], b1, b2)):
        same = zones == zones[0:1]
        for at, cond in ((0, same), (cy - 1, jnp.logical_not(same))):
            v1 = jnp.sum(jnp.where(cond, t1, 0.0), axis=0, keepdims=True)
            v2 = jnp.sum(jnp.where(cond, t2, 0.0), axis=0, keepdims=True)
            k = look_up(slots, jnp.broadcast_to(zones[at:at + 1], (8, 128)))[0:1]
            own_by, part = k // per, k % per
            w = jnp.where(owner == own_by, 1.0, 0.0).astype(F32)
            v = jnp.where(sub == part, v1, jnp.where(sub == part + per, v2, 0.0))
            out = out + lax.dot_general(w, v, (((1,), (1,)), ((), ())),
                                        precision=lax.Precision.HIGHEST, preferred_element_type=F32)
    lane16 = lax.broadcasted_iota(jnp.int32, (n, 16), 1)
    for j, value in enumerate((bb, bq, qq, energy)):
        value = jnp.sum(jnp.sum(value, axis=0, keepdims=True), axis=1, keepdims=True)
        out = jnp.where(lane16 == 2 * per + j, value, out)
    MS[...] = jnp.zeros_like(MS)
    MS[:, 0, 0:16] = out

    for a, b, c in offsets:
        there = (xs[a], ys[b], zs[c])
        t = (there[0] * ny + there[1]) * nz + there[2]
        pltpu.make_async_remote_copy(
            src_ref=MS.at[t], dst_ref=R.at[slot_at(a, b, c)], send_sem=rs_send, recv_sem=rs_recv,
            device_id=there, device_id_type=MESH).start()
    pltpu.make_async_copy(R, R, rs_recv).wait()
    pltpu.make_async_copy(R, R, rs_send).wait()
    row = jnp.sum(R[:, 0, :], axis=0, keepdims=True) + MS[me]

    def pick(j):
        return jnp.sum(jnp.where(lane1 == 2 * per + j, row, 0.0), axis=1, keepdims=True)
    bb, bq, qq, qkq = pick(0), pick(1), pick(2), pick(3)
    gram = bb * qq - bq * bq
    top = SPRING * gram + (bb * qkq - bq * qq)
    det = SPRING * top + (bq * qkq - qq * qq)
    plane = det != 0.0
    c1 = jnp.where(plane, top / det, bb / (SPRING * bb + bq))
    c2 = jnp.where(plane, -gram / det, 0.0)
    both = c1 * row + c2 * pltpu.roll(row, 128 - per, 1)
    grad_ref[...] = both[:, 0:per]

    def finish(x, carry):
        for k in range(3):
            adj_ref[k, x] = c1 * load[k, x] + c2 * Q[k, x]
        return carry
    lax.fori_loop(0, cx, finish, 0)


def solution(mesh):
    sizes = (mesh.shape["gx"], mesh.shape["gy"], mesh.shape["gz"])
    n = sizes[0] * sizes[1] * sizes[2]

    def on_device(displacement, adjoint_load, bone_mask, elem_zone, zone_slot, zone_modulus):
        cx, cy, cz = bone_mask.shape
        per = zone_modulus.shape[0]
        wy, wz = cy + 8, 2 * cz
        vm = pl.BlockSpec(memory_space=pltpu.VMEM)
        rows = zone_slot.shape[0] // 128
        scratch = [
            (8, cx + 3, wy, wz), (12, cx + 3, wy, wz), (12, cx + 1, cy, cz), (12, cx + 3, wy, wz),
            (3, cx + 1, cy, cz), (12, cx + 1, cy, cz), (2, cx + 2, cy, cz),
            (n, 1, 128), (n, 1, 128), (n - 1, 1, 128),
            (cy, 128), (cy, 128), (cy, 128), (cy, 128),
            (11, cx, wz), (LOW, cx, wz), (LOW, cx, wz), (11, cx, wz),
        ]
        adjoint, gradient = pl.pallas_call(
            functools.partial(kernel, sizes),
            out_shape=(jax.ShapeDtypeStruct(adjoint_load.shape, F32), jax.ShapeDtypeStruct((1, per), F32)),
            in_specs=[pl.BlockSpec(memory_space=pltpu.HBM)] * 6,
            out_specs=(vm, vm),
            scratch_shapes=[
                pltpu.VMEM(displacement.shape, F32), pltpu.VMEM(adjoint_load.shape, F32),
                pltpu.VMEM(bone_mask.shape, jnp.int32), pltpu.VMEM(elem_zone.shape, jnp.int32),
                pltpu.VMEM((rows, 128), jnp.int32), pltpu.SMEM((per,), F32)]
            + [pltpu.VMEM(s, F32) for s in scratch]
            + [pltpu.SemaphoreType.DMA] * 4 + [pltpu.SemaphoreType.DMA((6,))] * 3,
            compiler_params=pltpu.CompilerParams(collective_id=0, has_side_effects=True, vmem_limit_bytes=60 * 2**20),
            cost_estimate=pl.CostEstimate(flops=10**7, bytes_accessed=10**6, transcendentals=0),
        )(displacement, adjoint_load, bone_mask, elem_zone, zone_slot.reshape(-1, 128), zone_modulus)
        return adjoint, gradient.reshape(per)

    whole = P(None, "gx", "gy", "gz")
    brick = P("gx", "gy", "gz")
    owned = P(("gx", "gy", "gz"))
    return jax.shard_map(on_device, mesh=mesh, in_specs=(whole, whole, brick, brick, P(), owned),
                         out_specs=(whole, owned), check_vma=False)
```

```python
import functools
import jax
import jax.numpy as jnp
from jax import lax
from jax.experimental import pallas as pl
from jax.experimental.pallas import tpu as pltpu
from jax.sharding import PartitionSpec as P

ZS = 16
SPRING = 0.1
MESH = pl.DeviceIdType.MESH
LAME = 0.3 / (1.3 * 0.4)
SHEAR = 0.5 / 1.3
F32 = jnp.float32
LOW = 5


def element_forces(m):
    c = 1.0 / 16.0
    lam, mu = c * LAME, c * SHEAR
    lam3, mu3 = lam / 3.0, mu / 3.0
    u, v, w = m
    f = [[[[None, None], [None, None]], [[None, None], [None, None]]] for _ in range(3)]
    div = lam * (u[1][0][0] + v[0][1][0] + w[0][0][1])
    f[0][1][0][0] = div + (2 * mu) * u[1][0][0]
    f[1][0][1][0] = div + (2 * mu) * v[0][1][0]
    f[2][0][0][1] = div + (2 * mu) * w[0][0][1]
    f[0][0][1][0] = f[1][1][0][0] = mu * (u[0][1][0] + v[1][0][0])
    f[1][0][0][1] = f[2][0][1][0] = mu * (v[0][0][1] + w[0][1][0])
    f[0][0][0][1] = f[2][1][0][0] = mu * (u[0][0][1] + w[1][0][0])
    t = lam3 * (u[1][1][0] + w[0][1][1])
    f[0][1][1][0] = t + mu * u[1][1][0]
    f[2][0][1][1] = t + mu * w[0][1][1]
    t = lam3 * (u[1][0][1] + v[0][1][1])
    f[0][1][0][1] = t + mu * u[1][0][1]
    f[1][0][1][1] = t + mu * v[0][1][1]
    t = lam3 * (v[1][1][0] + w[1][0][1])
    f[1][1][1][0] = t + mu * v[1][1][0]
    f[2][1][0][1] = t + mu * w[1][0][1]
    t = u[0][1][1] + v[1][0][1] + w[1][1][0]
    f[0][0][1][1] = mu3 * (t + u[0][1][1])
    f[1][1][0][1] = mu3 * (t + v[1][0][1])
    f[2][1][1][0] = mu3 * (t + w[1][1][0])
    for k in range(3):
        f[k][1][1][1] = ((lam + 4 * mu) / 9.0) * m[k][1][1][1]
    return f


def modes_of(load, x):
    out = []
    for k in range(3):
        here = [[load(4 * k + 2 * b + c, x) for c in range(2)] for b in range(2)]
        there = [[load(4 * k + 2 * b + c, x + 1) for c in range(2)] for b in range(2)]
        out.append([
            [[None if b + c == 0 else there[b][c] + here[b][c] for c in range(2)] for b in range(2)],
            [[there[b][c] - here[b][c] for c in range(2)] for b in range(2)],
        ])
    return out


ALL = [(k, a, b, c) for k in range(3) for a in range(2) for b in range(2) for c in range(2) if a + b + c]


def dot_modes(f, g):
    total = None
    for k, a, b, c in ALL:
        t = f[k][a][b][c] * g[k][a][b][c]
        total = t if total is None else total + t
    return total


def kernel(sizes, disp_in, load_in, mask_in, zone_in, slot_in, mod_in, adj_ref, grad_ref,
           disp, load, mask, zone, slot_ref, mod_ref,
           E, BM, DM, NB, Q, QM, TB, G, MS, R, ZPL, ZPH, ZL, ZH, YPL, YPH, YL, YH,
           ag_send, ag_recv, rs_send, rs_recv, hs, hr, ins):
    nx, ny, nz = sizes
    n = nx * ny * nz
    cx, cy, cz = mask.shape
    wy, wz = cy + 8, 2 * cz
    per = mod_ref.shape[0]
    rows = slot_ref.shape[0]
    ix, iy, iz = lax.axis_index("gx"), lax.axis_index("gy"), lax.axis_index("gz")
    me = (ix * ny + iy) * nz + iz

    barrier = pltpu.get_barrier_semaphore()
    offsets = [(a, b, c) for a in range(nx) for b in range(ny) for c in range(nz)][1:]

    def around(spot, step, count):
        if step == 0:
            return spot
        there = spot + step
        return jnp.where(there >= count, there - count, there)
    xs = [around(ix, a, nx) for a in range(nx)]
    ys = [around(iy, b, ny) for b in range(ny)]
    zs = [around(iz, c, nz) for c in range(nz)]

    def slot_at(a, b, c):
        return ((-a % nx) * ny + (-b % ny)) * nz + (-c % nz) - 1

    for a, b, c in offsets:
        pl.semaphore_signal(barrier, inc=1, device_id=(xs[a], ys[b], zs[c]), device_id_type=MESH)
    copies = [pltpu.make_async_copy(src, dst, ins.at[i]) for i, (src, dst) in enumerate(
        ((mod_in, mod_ref), (load_in, load), (mask_in, mask), (zone_in, zone), (disp_in, disp),
         (slot_in, slot_ref)))]
    for copy in copies:
        copy.start()
    for copy in copies:
        copy.wait()

    lane1 = lax.broadcasted_iota(jnp.int32, (1, 128), 1)
    row = jnp.zeros((1, 128), F32)
    for j in range(per):
        row = jnp.where(lane1 == (me * per) % 128 + j, mod_ref[j], row)
    G[me] = row

    def remote(src, dst, send, recv, device):
        return pltpu.make_async_remote_copy(
            src_ref=src, dst_ref=dst, send_sem=hs.at[send], recv_sem=hr.at[recv],
            device_id=device, device_id_type=MESH)

    def links(entries):
        for out, target, dst, _, source in entries:
            pl.when(target)(out.start)

            @pl.when(jnp.logical_not(source))
            def _(dst=dst):
                dst[...] = jnp.zeros(dst.shape, F32)

        def finish():
            for out, target, dst, sem, source in entries:
                pl.when(target)(out.wait_send)
                pl.when(source)(pltpu.make_async_copy(dst, dst, hr.at[sem]).wait)
        return finish

    def has(spot, step, count):
        return jnp.logical_and(spot + step >= 0, spot + step < count)

    def near(spot, step, count):
        return jnp.clip(spot + step, 0, count - 1)

    lane = lax.broadcasted_iota(jnp.int32, (cy, 128), 1)

    def fill(x, carry):
        low, high = carry
        for f in range(8):
            if f < 3:
                value = load[f, x]
            elif f == 3:
                value = mask[x].astype(F32)
            elif f == 4:
                value = zone[x].astype(F32)
            else:
                value = disp[f - 5, x]
            E[f, x + 1, 0:cy, 0:cz] = value
            low = jnp.where(lane == f * 8 + x, pltpu.roll(value, f * 8 + x, 1), low)
            if f < 3:
                low = jnp.where(lane == (8 + f) * 8 + x, pltpu.roll(value, (8 + f) * 8 + x - 1, 1), low)
            if f < LOW:
                high = jnp.where(lane == f * 8 + x, pltpu.roll(value, f * 8 + x + 1, 1), high)
        return low, high
    zero = jnp.zeros((cy, 128), F32)
    low, high = lax.fori_loop(0, cx, fill, (zero, zero))
    ZPL[...] = low
    ZPH[...] = high
    for f in range(8):
        YPL[f] = E[f, 1:cx + 1, 0, 0:cz]
        if f < 3:
            YPL[8 + f] = E[f, 1:cx + 1, 1, 0:cz]
        if f < LOW:
            YPH[f] = E[f, 1:cx + 1, cy - 1, 0:cz]
    pl.semaphore_wait(barrier, n - 1)
    entries = []
    for d in (0, -1, 1):
        for side, src, dst, step in ((0, ZPL, ZH, -1), (1, ZPH, ZL, 1)):
            target = jnp.logical_and(has(iy, d, ny), has(iz, step, nz))
            source = jnp.logical_and(has(iy, d, ny), has(iz, -step, nz))
            out = remote(src, dst.at[1 - d], 3 * side + 1 + d, 3 * side + 1 - d,
                         {"gy": near(iy, d, ny), "gz": near(iz, step, nz)})
            entries.append((out, target, dst.at[1 + d], 3 * side + 1 + d, source))
    for s, src, dst, step in ((6, YPL, YH, -1), (7, YPH, YL, 1)):
        out = remote(src, dst, s, s, {"gy": near(iy, step, ny)})
        entries.append((out, has(iy, step, ny), dst, s, has(iy, -step, ny)))
    finish_zy = links(entries)
    for a, b, c in offsets:
        pltpu.make_async_remote_copy(
            src_ref=G.at[me], dst_ref=G.at[me], send_sem=ag_send, recv_sem=ag_recv,
            device_id=(xs[a], ys[b], zs[c]), device_id_type=MESH).start()
    for i in range(12):
        NB[i, 1] = jnp.zeros((wy, wz), F32)
    finish_zy()

    line = lax.broadcasted_iota(jnp.int32, (8, 128), 0)
    tall = lax.broadcasted_iota(jnp.int32, (wy, 128), 1)

    def corners(ref):
        return jnp.concatenate([ref[1], jnp.where(
            line == 7, ref[0, cy - 8:cy], jnp.where(line < 2, ref[2, 0:8], 0.0))], axis=0)
    above_z, below_z = corners(ZH), corners(ZL)

    def open_z(x, carry):
        above, below = carry
        for f in range(8):
            tile = jnp.where(tall == 0, pltpu.roll(above, 128 - f * 8 - x, 1), 0.0)
            if f < 3:
                tile = jnp.where(tall == 1, pltpu.roll(above, 128 + 1 - (8 + f) * 8 - x, 1), tile)
            if f < LOW:
                tile = jnp.where(tall == 127, pltpu.roll(below, 127 - f * 8 - x, 1), tile)
            E[f, x + 1, :, cz:wz] = tile
        return carry
    lax.fori_loop(0, cx, open_z, (above_z, below_z))
    for f in range(8):
        above = YH[f]
        second = YH[8 + f] if f < 3 else None
        below = YL[f] if f < LOW else None
        for x in range(cx):
            tile = jnp.where(line == 0, above[x:x + 1], 0.0)
            if f < 3:
                tile = jnp.where(line == 1, second[x:x + 1], tile)
            if f < LOW:
                tile = jnp.where(line == 7, below[x:x + 1], tile)
            E[f, x + 1, cy:wy, 0:cz] = tile
    finish_x = links([
        (remote(E.at[:, pl.ds(1, 2)], E.at[:, pl.ds(cx + 1, 2)], 8, 8, {"gx": near(ix, -1, nx)}),
         has(ix, -1, nx), E.at[:, pl.ds(cx + 1, 2)], 8, has(ix, 1, nx)),
        (remote(E.at[pl.ds(0, LOW), pl.ds(cx, 1)], E.at[pl.ds(0, LOW), pl.ds(0, 1)], 9, 9,
                {"gx": near(ix, 1, nx)}),
         has(ix, 1, nx), E.at[pl.ds(0, LOW), pl.ds(0, 1)], 9, has(ix, -1, nx)),
    ])

    def yz_modes(v, put, x, k):
        after = pltpu.roll(v, wz - 1, 1)
        for c, t in enumerate((v + after, after - v)):
            above = pltpu.roll(t, wy - 1, 0)
            put(4 * k + c, x, t + above)
            put(4 * k + 2 + c, x, above - t)

    def put_b(i, x, v):
        BM[i, x] = v

    def put_d(i, x, v):
        DM[i, x] = v[0:cy, 0:cz]

    def put_q(i, x, v):
        QM[i, x] = v[0:cy, 0:cz]

    def b_modes(x, carry):
        for k in range(3):
            yz_modes(E[k, x], put_b, x, k)
        return carry

    def d_modes(x, carry):
        for k in range(3):
            yz_modes(E[5 + k, x + 1], put_d, x, k)
        return carry

    lax.fori_loop(0, cx, d_modes, 0)
    lax.fori_loop(1, cx + 1, b_modes, 0)

    whole = G.at[pl.ds(0, n - 1)]
    pltpu.make_async_copy(whole, whole, ag_recv).wait()
    pltpu.make_async_copy(whole, whole, ag_send).wait()
    group = n // rows
    by_slot = [jnp.sum(G[g * group:(g + 1) * group, 0, :], axis=0, keepdims=True) for g in range(rows)]

    def look_up(tables, index):
        tables = [jnp.broadcast_to(t, (8, 128)) for t in tables]
        low_bits, which = index % 128, index // 128
        out = None
        for g, t in enumerate(tables):
            got = jnp.take_along_axis(t, low_bits, axis=1, mode="promise_in_bounds")
            out = got if out is None else jnp.where(which == g, got, out)
        return out
    by_zone = []
    for g in range(rows):
        index = jnp.broadcast_to(slot_ref[g:g + 1, :], (8, 128))
        by_zone.append(look_up(by_slot, index)[0:1])

    def first(x, carry, lowest=False):
        where = E[4, x].astype(jnp.int32)
        parts = []
        for y in range(0, wy, 8):
            parts.append(jnp.concatenate(
                [look_up(by_zone, where[y:y + 8, z:z + 128]) for z in range(0, wz, 128)], axis=1))
        stiff = jnp.where(E[3, x] > 0.5, jnp.concatenate(parts, axis=0), 0.0)
        TB[1, x] = stiff[0:cy, 0:cz]
        f = element_forces(modes_of(lambda i, p: BM[i, p], x))

        def terms():
            inner = [[[[None if t is None else t[0:cy, 0:cz] for t in b] for b in a] for a in k] for k in f]
            TB[0, x] = dot_modes(inner, modes_of(lambda i, p: DM[i, p], x - 1))
        if not lowest:
            pl.when(x <= cx)(terms)
        for k in range(3):
            for b in range(2):
                for c in range(2):
                    i = 4 * k + 2 * b + c
                    delta = f[k][1][b][c] * stiff
                    if b + c:
                        total = f[k][0][b][c] * stiff
                        now, later = total - delta, total + delta
                    else:
                        now, later = -delta, delta
                    if lowest:
                        NB[i, 1] = NB[i, 1] + later
                    else:
                        NB[i, x] = NB[i, x] + now
                        NB[i, x + 1] = later
        return carry
    lax.fori_loop(1, cx, first, 0)
    finish_x()
    b_modes(0, 0)
    lax.fori_loop(cx + 1, cx + 3, b_modes, 0)
    d_modes(cx, 0)
    lax.fori_loop(cx, cx + 2, first, 0)
    first(0, 0, lowest=True)

    at_y = lax.broadcasted_iota(jnp.int32, (wy, wz), 0)
    at_z = lax.broadcasted_iota(jnp.int32, (wy, wz), 1)
    last_x, last_y, last_z = ix == nx - 1, iy == ny - 1, iz == nz - 1
    keep_y = jnp.where(last_y, cy, wy)
    keep_z = jnp.where(last_z, cz, wz)
    inside = jnp.logical_and(at_y < keep_y, at_z < keep_z)

    def nodes(x, carry):
        bq, qq, bb = carry
        keep_x = jnp.where(last_x, cx, cx + 1)
        valid = jnp.logical_and(inside, jnp.broadcast_to(x, (wy, wz)) < keep_x)
        own = jnp.where(x < cx, 1.0, 0.0).astype(F32)
        for k in range(3):
            side = []
            for c in range(2):
                s, d = NB[4 * k + c, x + 1], NB[4 * k + 2 + c, x + 1]
                side.append((s - d) + pltpu.roll(s + d, 1, 0))
            q = (side[0] - side[1]) + pltpu.roll(side[0] + side[1], 1, 1)
            q = jnp.where(valid, q, 0.0)
            mine = q[0:cy, 0:cz]
            Q[k, x] = mine
            v = E[k, x + 1, 0:cy, 0:cz]
            bq = bq + own * (v * mine)
            qq = qq + own * (mine * mine)
            bb = bb + own * (v * v)
            yz_modes(q, put_q, x, k)
        return bq, qq, bb
    bq, qq, bb = lax.fori_loop(0, cx + 1, nodes, (zero, zero, zero))

    scale = -(ZS ** -1.5)
    first_zone = zone[0]

    def second(x, carry):
        energy, a1, a2, b1, b2 = carry
        m = modes_of(lambda i, p: QM[i, p], x)
        f = element_forces(m)
        energy = energy + TB[1, x + 1] * dot_modes(f, m)
        bone = scale * mask[x].astype(F32)
        t2 = bone * dot_modes(f, modes_of(lambda i, p: DM[i, p], x))
        t1 = bone * TB[0, x + 1]
        same = zone[x] == first_zone
        a1 = a1 + jnp.where(same, t1, 0.0)
        a2 = a2 + jnp.where(same, t2, 0.0)
        b1 = b1 + jnp.where(same, 0.0, t1)
        b2 = b2 + jnp.where(same, 0.0, t2)
        return energy, a1, a2, b1, b2
    energy, a1, a2, b1, b2 = lax.fori_loop(0, cx, second, (zero,) * 5)

    owner = lax.broadcasted_iota(jnp.int32, (n, 128), 0)
    sub = lax.broadcasted_iota(jnp.int32, (16, 128), 0)
    slots = [slot_ref[g:g + 1, :] for g in range(rows)]
    out = jnp.zeros((n, 16), F32)
    for zones, t1, t2 in ((first_zone, a1, a2), (zone[cx - 1], b1, b2)):
        same = zones == zones[0:1]
        for at, cond in ((0, same), (cy - 1, jnp.logical_not(same))):
            v1 = jnp.sum(jnp.where(cond, t1, 0.0), axis=0, keepdims=True)
            v2 = jnp.sum(jnp.where(cond, t2, 0.0), axis=0, keepdims=True)
            k = look_up(slots, jnp.broadcast_to(zones[at:at + 1], (8, 128)))[0:1]
            own_by, part = k // per, k % per
            w = jnp.where(owner == own_by, 1.0, 0.0).astype(F32)
            v = jnp.where(sub == part, v1, jnp.where(sub == part + per, v2, 0.0))
            out = out + lax.dot_general(w, v, (((1,), (1,)), ((), ())),
                                        precision=lax.Precision.HIGHEST, preferred_element_type=F32)
    lane16 = lax.broadcasted_iota(jnp.int32, (n, 16), 1)
    for j, value in enumerate((bb, bq, qq, energy)):
        value = jnp.sum(jnp.sum(value, axis=0, keepdims=True), axis=1, keepdims=True)
        out = jnp.where(lane16 == 2 * per + j, value, out)
    MS[...] = jnp.zeros_like(MS)
    MS[:, 0, 0:16] = out

    for a, b, c in offsets:
        there = (xs[a], ys[b], zs[c])
        t = (there[0] * ny + there[1]) * nz + there[2]
        pltpu.make_async_remote_copy(
            src_ref=MS.at[t], dst_ref=R.at[slot_at(a, b, c)], send_sem=rs_send, recv_sem=rs_recv,
            device_id=there, device_id_type=MESH).start()
    pltpu.make_async_copy(R, R, rs_recv).wait()
    pltpu.make_async_copy(R, R, rs_send).wait()
    row = jnp.sum(R[:, 0, :], axis=0, keepdims=True) + MS[me]

    def pick(j):
        return jnp.sum(jnp.where(lane1 == 2 * per + j, row, 0.0), axis=1, keepdims=True)
    bb, bq, qq, qkq = pick(0), pick(1), pick(2), pick(3)
    gram = bb * qq - bq * bq
    top = SPRING * gram + (bb * qkq - bq * qq)
    det = SPRING * top + (bq * qkq - qq * qq)
    plane = det != 0.0
    c1 = jnp.where(plane, top / det, bb / (SPRING * bb + bq))
    c2 = jnp.where(plane, -gram / det, 0.0)
    both = c1 * row + c2 * pltpu.roll(row, 128 - per, 1)
    grad_ref[...] = both[:, 0:per]

    def finish(x, carry):
        for k in range(3):
            adj_ref[k, x] = c1 * load[k, x] + c2 * Q[k, x]
        return carry
    lax.fori_loop(0, cx, finish, 0)


def solution(mesh):
    sizes = (mesh.shape["gx"], mesh.shape["gy"], mesh.shape["gz"])
    n = sizes[0] * sizes[1] * sizes[2]

    def on_device(displacement, adjoint_load, bone_mask, elem_zone, zone_slot, zone_modulus):
        cx, cy, cz = bone_mask.shape
        per = zone_modulus.shape[0]
        wy, wz = cy + 8, 2 * cz
        vm = pl.BlockSpec(memory_space=pltpu.VMEM)
        rows = zone_slot.shape[0] // 128
        scratch = [
            (8, cx + 3, wy, wz), (12, cx + 3, wy, wz), (12, cx + 1, cy, cz), (12, cx + 3, wy, wz),
            (3, cx + 1, cy, cz), (12, cx + 1, cy, cz), (2, cx + 2, cy, cz),
            (n, 1, 128), (n, 1, 128), (n - 1, 1, 128),
            (cy, 128), (cy, 128), (3, cy, 128), (3, cy, 128),
            (11, cx, cz), (LOW, cx, cz), (LOW, cx, cz), (11, cx, cz),
        ]
        adjoint, gradient = pl.pallas_call(
            functools.partial(kernel, sizes),
            out_shape=(jax.ShapeDtypeStruct(adjoint_load.shape, F32), jax.ShapeDtypeStruct((1, per), F32)),
            in_specs=[pl.BlockSpec(memory_space=pltpu.HBM)] * 6,
            out_specs=(vm, vm),
            scratch_shapes=[
                pltpu.VMEM(displacement.shape, F32), pltpu.VMEM(adjoint_load.shape, F32),
                pltpu.VMEM(bone_mask.shape, jnp.int32), pltpu.VMEM(elem_zone.shape, jnp.int32),
                pltpu.VMEM((rows, 128), jnp.int32), pltpu.SMEM((per,), F32)]
            + [pltpu.VMEM(s, F32) for s in scratch]
            + [pltpu.SemaphoreType.DMA] * 4 + [pltpu.SemaphoreType.DMA((10,))] * 2 + [pltpu.SemaphoreType.DMA((6,))],
            compiler_params=pltpu.CompilerParams(collective_id=0, has_side_effects=True, vmem_limit_bytes=60 * 2**20),
            cost_estimate=pl.CostEstimate(flops=10**7, bytes_accessed=10**6, transcendentals=0),
        )(displacement, adjoint_load, bone_mask, elem_zone, zone_slot.reshape(-1, 128), zone_modulus)
        return adjoint, gradient.reshape(per)

    whole = P(None, "gx", "gy", "gz")
    brick = P("gx", "gy", "gz")
    owned = P(("gx", "gy", "gz"))
    return jax.shard_map(on_device, mesh=mesh, in_specs=(whole, whole, brick, brick, P(), owned),
                         out_specs=(whole, owned), check_vma=False)
```

```python
import functools
import jax
import jax.numpy as jnp
from jax import lax
from jax.experimental import pallas as pl
from jax.experimental.pallas import tpu as pltpu
from jax.sharding import PartitionSpec as P

ZS = 16
SPRING = 0.1
MESH = pl.DeviceIdType.MESH
LAME = 0.3 / (1.3 * 0.4)
SHEAR = 0.5 / 1.3
F32 = jnp.float32
LOW = 5


def element_forces(m):
    c = 1.0 / 16.0
    lam, mu = c * LAME, c * SHEAR
    lam3, mu3 = lam / 3.0, mu / 3.0
    u, v, w = m
    f = [[[[None, None], [None, None]], [[None, None], [None, None]]] for _ in range(3)]
    div = lam * (u[1][0][0] + v[0][1][0] + w[0][0][1])
    f[0][1][0][0] = div + (2 * mu) * u[1][0][0]
    f[1][0][1][0] = div + (2 * mu) * v[0][1][0]
    f[2][0][0][1] = div + (2 * mu) * w[0][0][1]
    f[0][0][1][0] = f[1][1][0][0] = mu * (u[0][1][0] + v[1][0][0])
    f[1][0][0][1] = f[2][0][1][0] = mu * (v[0][0][1] + w[0][1][0])
    f[0][0][0][1] = f[2][1][0][0] = mu * (u[0][0][1] + w[1][0][0])
    t = lam3 * (u[1][1][0] + w[0][1][1])
    f[0][1][1][0] = t + mu * u[1][1][0]
    f[2][0][1][1] = t + mu * w[0][1][1]
    t = lam3 * (u[1][0][1] + v[0][1][1])
    f[0][1][0][1] = t + mu * u[1][0][1]
    f[1][0][1][1] = t + mu * v[0][1][1]
    t = lam3 * (v[1][1][0] + w[1][0][1])
    f[1][1][1][0] = t + mu * v[1][1][0]
    f[2][1][0][1] = t + mu * w[1][0][1]
    t = u[0][1][1] + v[1][0][1] + w[1][1][0]
    f[0][0][1][1] = mu3 * (t + u[0][1][1])
    f[1][1][0][1] = mu3 * (t + v[1][0][1])
    f[2][1][1][0] = mu3 * (t + w[1][1][0])
    for k in range(3):
        f[k][1][1][1] = ((lam + 4 * mu) / 9.0) * m[k][1][1][1]
    return f


def modes_of(load, x):
    out = []
    for k in range(3):
        here = [[load(4 * k + 2 * b + c, x) for c in range(2)] for b in range(2)]
        there = [[load(4 * k + 2 * b + c, x + 1) for c in range(2)] for b in range(2)]
        out.append([
            [[None if b + c == 0 else there[b][c] + here[b][c] for c in range(2)] for b in range(2)],
            [[there[b][c] - here[b][c] for c in range(2)] for b in range(2)],
        ])
    return out


ALL = [(k, a, b, c) for k in range(3) for a in range(2) for b in range(2) for c in range(2) if a + b + c]


def dot_modes(f, g):
    total = None
    for k, a, b, c in ALL:
        t = f[k][a][b][c] * g[k][a][b][c]
        total = t if total is None else total + t
    return total


def kernel(sizes, disp_in, load_in, mask_in, zone_in, slot_in, mod_in, adj_ref, grad_ref,
           disp, load, mask, zone, slot_ref, mod_ref,
           E, BM, DM, NB, Q, QM, TB, G, MS, R, ZPL, ZPH, ZL, ZH, YPL, YPH, YL, YH,
           ag_send, ag_recv, rs_send, rs_recv, hs, hr, ins):
    nx, ny, nz = sizes
    n = nx * ny * nz
    cx, cy, cz = mask.shape
    wy, wz = cy + 8, 2 * cz
    per = mod_ref.shape[0]
    rows = slot_ref.shape[0]
    ix, iy, iz = lax.axis_index("gx"), lax.axis_index("gy"), lax.axis_index("gz")
    me = (ix * ny + iy) * nz + iz

    barrier = pltpu.get_barrier_semaphore()
    offsets = [(a, b, c) for a in range(nx) for b in range(ny) for c in range(nz)][1:]

    def around(spot, step, count):
        if step == 0:
            return spot
        there = spot + step
        return jnp.where(there >= count, there - count, there)
    xs = [around(ix, a, nx) for a in range(nx)]
    ys = [around(iy, b, ny) for b in range(ny)]
    zs = [around(iz, c, nz) for c in range(nz)]

    def slot_at(a, b, c):
        return ((-a % nx) * ny + (-b % ny)) * nz + (-c % nz) - 1

    for a, b, c in offsets:
        pl.semaphore_signal(barrier, inc=1, device_id=(xs[a], ys[b], zs[c]), device_id_type=MESH)
    copies = [pltpu.make_async_copy(src, dst, ins.at[i]) for i, (src, dst) in enumerate(
        ((mod_in, mod_ref), (load_in, load), (mask_in, mask), (zone_in, zone), (disp_in, disp),
         (slot_in, slot_ref)))]
    for copy in copies:
        copy.start()
    for copy in copies:
        copy.wait()

    lane1 = lax.broadcasted_iota(jnp.int32, (1, 128), 1)
    row = jnp.zeros((1, 128), F32)
    for j in range(per):
        row = jnp.where(lane1 == (me * per) % 128 + j, mod_ref[j], row)
    G[me] = row

    def remote(src, dst, send, recv, device):
        return pltpu.make_async_remote_copy(
            src_ref=src, dst_ref=dst, send_sem=hs.at[send], recv_sem=hr.at[recv],
            device_id=device, device_id_type=MESH)

    def links(entries):
        for out, target, dst, _, source in entries:
            pl.when(target)(out.start)

            @pl.when(jnp.logical_not(source))
            def _(dst=dst):
                dst[...] = jnp.zeros(dst.shape, F32)

        def finish():
            for out, target, dst, sem, source in entries:
                pl.when(target)(out.wait_send)
                pl.when(source)(pltpu.make_async_copy(dst, dst, hr.at[sem]).wait)
        return finish

    def has(spot, step, count):
        return jnp.logical_and(spot + step >= 0, spot + step < count)

    def near(spot, step, count):
        return jnp.clip(spot + step, 0, count - 1)

    lane = lax.broadcasted_iota(jnp.int32, (cy, 128), 1)

    def fill(x, carry):
        low, high = carry
        for f in range(8):
            if f < 3:
                value = load[f, x]
            elif f == 3:
                value = mask[x].astype(F32)
            elif f == 4:
                value = zone[x].astype(F32)
            else:
                value = disp[f - 5, x]
            E[f, x + 1, 0:cy, 0:cz] = value
            low = jnp.where(lane == f * 8 + x, pltpu.roll(value, f * 8 + x, 1), low)
            if f < 3:
                low = jnp.where(lane == (8 + f) * 8 + x, pltpu.roll(value, (8 + f) * 8 + x - 1, 1), low)
            if f < LOW:
                high = jnp.where(lane == f * 8 + x, pltpu.roll(value, f * 8 + x + 1, 1), high)
        return low, high
    zero = jnp.zeros((cy, 128), F32)
    low, high = lax.fori_loop(0, cx, fill, (zero, zero))
    ZPL[...] = low
    ZPH[...] = high
    for f in range(8):
        YPL[f] = E[f, 1:cx + 1, 0, 0:cz]
        if f < 3:
            YPL[8 + f] = E[f, 1:cx + 1, 1, 0:cz]
        if f < LOW:
            YPH[f] = E[f, 1:cx + 1, cy - 1, 0:cz]
    pl.semaphore_wait(barrier, n - 1)
    entries = []
    for d in (0, -1, 1):
        for side, src, dst, step in ((0, ZPL, ZH, -1), (1, ZPH, ZL, 1)):
            target = jnp.logical_and(has(iy, d, ny), has(iz, step, nz))
            source = jnp.logical_and(has(iy, d, ny), has(iz, -step, nz))
            out = remote(src, dst.at[1 - d], 3 * side + 1 + d, 3 * side + 1 - d,
                         {"gy": near(iy, d, ny), "gz": near(iz, step, nz)})
            entries.append((out, target, dst.at[1 + d], 3 * side + 1 + d, source))
    for s, src, dst, step in ((6, YPL, YH, -1), (7, YPH, YL, 1)):
        out = remote(src, dst, s, s, {"gy": near(iy, step, ny)})
        entries.append((out, has(iy, step, ny), dst, s, has(iy, -step, ny)))
    finish_zy = links(entries)
    for a, b, c in offsets:
        pltpu.make_async_remote_copy(
            src_ref=G.at[me], dst_ref=G.at[me], send_sem=ag_send, recv_sem=ag_recv,
            device_id=(xs[a], ys[b], zs[c]), device_id_type=MESH).start()
    for i in range(12):
        NB[i, 1] = jnp.zeros((wy, wz), F32)
    finish_zy()

    line = lax.broadcasted_iota(jnp.int32, (8, 128), 0)
    tall = lax.broadcasted_iota(jnp.int32, (wy, 128), 1)

    def corners(ref):
        return jnp.concatenate([ref[1], jnp.where(
            line == 7, ref[0, cy - 8:cy], jnp.where(line < 2, ref[2, 0:8], 0.0))], axis=0)
    above_z, below_z = corners(ZH), corners(ZL)

    def open_z(x, carry):
        above, below = carry
        for f in range(8):
            tile = jnp.where(tall == 0, pltpu.roll(above, 128 - f * 8 - x, 1), 0.0)
            if f < 3:
                tile = jnp.where(tall == 1, pltpu.roll(above, 128 + 1 - (8 + f) * 8 - x, 1), tile)
            if f < LOW:
                tile = jnp.where(tall == 127, pltpu.roll(below, 127 - f * 8 - x, 1), tile)
            E[f, x + 1, :, cz:wz] = tile
        return carry
    lax.fori_loop(0, cx, open_z, (above_z, below_z))
    for f in range(8):
        above = YH[f]
        second = YH[8 + f] if f < 3 else None
        below = YL[f] if f < LOW else None
        for x in range(cx):
            tile = jnp.where(line == 0, above[x:x + 1], 0.0)
            if f < 3:
                tile = jnp.where(line == 1, second[x:x + 1], tile)
            if f < LOW:
                tile = jnp.where(line == 7, below[x:x + 1], tile)
            E[f, x + 1, cy:wy, 0:cz] = tile
    finish_x = links([
        (remote(E.at[:, pl.ds(1, 2)], E.at[:, pl.ds(cx + 1, 2)], 8, 8, {"gx": near(ix, -1, nx)}),
         has(ix, -1, nx), E.at[:, pl.ds(cx + 1, 2)], 8, has(ix, 1, nx)),
        (remote(E.at[pl.ds(0, LOW), pl.ds(cx, 1)], E.at[pl.ds(0, LOW), pl.ds(0, 1)], 9, 9,
                {"gx": near(ix, 1, nx)}),
         has(ix, 1, nx), E.at[pl.ds(0, LOW), pl.ds(0, 1)], 9, has(ix, -1, nx)),
    ])

    def yz_modes(v, put, x, k):
        after = pltpu.roll(v, wz - 1, 1)
        for c, t in enumerate((v + after, after - v)):
            above = pltpu.roll(t, wy - 1, 0)
            put(4 * k + c, x, t + above)
            put(4 * k + 2 + c, x, above - t)

    def put_b(i, x, v):
        BM[i, x] = v

    def put_d(i, x, v):
        DM[i, x] = v[0:cy, 0:cz]

    def put_q(i, x, v):
        QM[i, x] = v[0:cy, 0:cz]

    def b_modes(x, carry):
        for k in range(3):
            yz_modes(E[k, x], put_b, x, k)
        return carry

    def d_modes(x, carry):
        for k in range(3):
            yz_modes(E[5 + k, x + 1], put_d, x, k)
        return carry

    lax.fori_loop(0, cx, d_modes, 0)
    lax.fori_loop(1, cx + 1, b_modes, 0)

    whole = G.at[pl.ds(0, n - 1)]
    pltpu.make_async_copy(whole, whole, ag_recv).wait()
    pltpu.make_async_copy(whole, whole, ag_send).wait()
    group = n // rows
    by_slot = [jnp.sum(G[g * group:(g + 1) * group, 0, :], axis=0, keepdims=True) for g in range(rows)]

    def look_up(tables, index):
        tables = [jnp.broadcast_to(t, (8, 128)) for t in tables]
        low_bits, which = index % 128, index // 128
        out = None
        for g, t in enumerate(tables):
            got = jnp.take_along_axis(t, low_bits, axis=1, mode="promise_in_bounds")
            out = got if out is None else jnp.where(which == g, got, out)
        return out
    by_zone = []
    for g in range(rows):
        index = jnp.broadcast_to(slot_ref[g:g + 1, :], (8, 128))
        by_zone.append(look_up(by_slot, index)[0:1])

    def first(x, carry, lowest=False):
        where = E[4, x].astype(jnp.int32)
        parts = []
        for y in range(0, wy, 8):
            parts.append(jnp.concatenate(
                [look_up(by_zone, where[y:y + 8, z:z + 128]) for z in range(0, wz, 128)], axis=1))
        stiff = jnp.where(E[3, x] > 0.5, jnp.concatenate(parts, axis=0), 0.0)
        TB[1, x] = stiff[0:cy, 0:cz]
        f = element_forces(modes_of(lambda i, p: BM[i, p], x))

        def terms():
            inner = [[[[None if t is None else t[0:cy, 0:cz] for t in b] for b in a] for a in k] for k in f]
            TB[0, x] = dot_modes(inner, modes_of(lambda i, p: DM[i, p], x - 1))
        if not lowest:
            pl.when(x <= cx)(terms)
        for k in range(3):
            for b in range(2):
                for c in range(2):
                    i = 4 * k + 2 * b + c
                    delta = f[k][1][b][c] * stiff
                    if b + c:
                        total = f[k][0][b][c] * stiff
                        now, later = total - delta, total + delta
                    else:
                        now, later = -delta, delta
                    if lowest:
                        NB[i, 1] = NB[i, 1] + later
                    else:
                        NB[i, x] = NB[i, x] + now
                        NB[i, x + 1] = later
        return carry
    lax.fori_loop(1, cx, first, 0)
    finish_x()
    b_modes(0, 0)
    lax.fori_loop(cx + 1, cx + 3, b_modes, 0)
    d_modes(cx, 0)
    lax.fori_loop(cx, cx + 2, first, 0)
    first(0, 0, lowest=True)

    at_y = lax.broadcasted_iota(jnp.int32, (wy, wz), 0)
    at_z = lax.broadcasted_iota(jnp.int32, (wy, wz), 1)
    last_x, last_y, last_z = ix == nx - 1, iy == ny - 1, iz == nz - 1
    keep_y = jnp.where(last_y, cy, wy)
    keep_z = jnp.where(last_z, cz, wz)
    inside = jnp.logical_and(at_y < keep_y, at_z < keep_z)

    def nodes(x, carry):
        bq, qq, bb = carry
        keep_x = jnp.where(last_x, cx, cx + 1)
        valid = jnp.logical_and(inside, jnp.broadcast_to(x, (wy, wz)) < keep_x)
        own = jnp.where(x < cx, 1.0, 0.0).astype(F32)
        for k in range(3):
            side = []
            for c in range(2):
                s, d = NB[4 * k + c, x + 1], NB[4 * k + 2 + c, x + 1]
                side.append((s - d) + pltpu.roll(s + d, 1, 0))
            q = (side[0] - side[1]) + pltpu.roll(side[0] + side[1], 1, 1)
            q = jnp.where(valid, q, 0.0)
            mine = q[0:cy, 0:cz]
            Q[k, x] = mine
            v = E[k, x + 1, 0:cy, 0:cz]
            bq = bq + own * (v * mine)
            qq = qq + own * (mine * mine)
            bb = bb + own * (v * v)
            yz_modes(q, put_q, x, k)
        return bq, qq, bb
    bq, qq, bb = lax.fori_loop(0, cx + 1, nodes, (zero, zero, zero))

    scale = -(ZS ** -1.5)
    first_zone = zone[0]

    def second(x, carry):
        energy, a1, a2, b1, b2 = carry
        m = modes_of(lambda i, p: QM[i, p], x)
        f = element_forces(m)
        energy = energy + TB[1, x + 1] * dot_modes(f, m)
        bone = scale * mask[x].astype(F32)
        t2 = bone * dot_modes(f, modes_of(lambda i, p: DM[i, p], x))
        t1 = bone * TB[0, x + 1]
        same = zone[x] == first_zone
        a1 = a1 + jnp.where(same, t1, 0.0)
        a2 = a2 + jnp.where(same, t2, 0.0)
        b1 = b1 + jnp.where(same, 0.0, t1)
        b2 = b2 + jnp.where(same, 0.0, t2)
        return energy, a1, a2, b1, b2
    energy, a1, a2, b1, b2 = lax.fori_loop(0, cx, second, (zero,) * 5)

    owner = lax.broadcasted_iota(jnp.int32, (n, 128), 0)
    sub = lax.broadcasted_iota(jnp.int32, (16, 128), 0)
    slots = [slot_ref[g:g + 1, :] for g in range(rows)]
    out = jnp.zeros((n, 16), F32)
    for zones, t1, t2 in ((first_zone, a1, a2), (zone[cx - 1], b1, b2)):
        same = zones == zones[0:1]
        for at, cond in ((0, same), (cy - 1, jnp.logical_not(same))):
            v1 = jnp.sum(jnp.where(cond, t1, 0.0), axis=0, keepdims=True)
            v2 = jnp.sum(jnp.where(cond, t2, 0.0), axis=0, keepdims=True)
            k = look_up(slots, jnp.broadcast_to(zones[at:at + 1], (8, 128)))[0:1]
            own_by, part = k // per, k % per
            w = jnp.where(owner == own_by, 1.0, 0.0).astype(F32)
            v = jnp.where(sub == part, v1, jnp.where(sub == part + per, v2, 0.0))
            out = out + lax.dot_general(w, v, (((1,), (1,)), ((), ())),
                                        precision=lax.Precision.HIGHEST, preferred_element_type=F32)
    lane16 = lax.broadcasted_iota(jnp.int32, (n, 16), 1)
    for j, value in enumerate((bb, bq, qq, energy)):
        value = jnp.sum(jnp.sum(value, axis=0, keepdims=True), axis=1, keepdims=True)
        out = jnp.where(lane16 == 2 * per + j, value, out)
    MS[...] = jnp.zeros_like(MS)
    MS[:, 0, 0:16] = out

    for a, b, c in offsets:
        there = (xs[a], ys[b], zs[c])
        t = (there[0] * ny + there[1]) * nz + there[2]
        pltpu.make_async_remote_copy(
            src_ref=MS.at[t], dst_ref=R.at[slot_at(a, b, c)], send_sem=rs_send, recv_sem=rs_recv,
            device_id=there, device_id_type=MESH).start()
    pltpu.make_async_copy(R, R, rs_recv).wait()
    pltpu.make_async_copy(R, R, rs_send).wait()
    row = jnp.sum(R[:, 0, :], axis=0, keepdims=True) + MS[me]

    def pick(j):
        return jnp.sum(jnp.where(lane1 == 2 * per + j, row, 0.0), axis=1, keepdims=True)
    bb, bq, qq, qkq = pick(0), pick(1), pick(2), pick(3)
    gram = bb * qq - bq * bq
    top = SPRING * gram + (bb * qkq - bq * qq)
    det = SPRING * top + (bq * qkq - qq * qq)
    plane = det != 0.0
    c1 = jnp.where(plane, top / det, bb / (SPRING * bb + bq))
    c2 = jnp.where(plane, -gram / det, 0.0)
    both = c1 * row + c2 * pltpu.roll(row, 128 - per, 1)
    grad_ref[...] = both[:, 0:per]

    def finish(x, carry):
        for k in range(3):
            adj_ref[k, x] = c1 * load[k, x] + c2 * Q[k, x]
        return carry
    lax.fori_loop(0, cx, finish, 0)


def solution(mesh):
    sizes = (mesh.shape["gx"], mesh.shape["gy"], mesh.shape["gz"])
    n = sizes[0] * sizes[1] * sizes[2]

    def on_device(displacement, adjoint_load, bone_mask, elem_zone, zone_slot, zone_modulus):
        cx, cy, cz = bone_mask.shape
        per = zone_modulus.shape[0]
        wy, wz = cy + 8, 2 * cz
        vm = pl.BlockSpec(memory_space=pltpu.VMEM)
        rows = zone_slot.shape[0] // 128
        scratch = [
            (8, cx + 3, wy, wz), (12, cx + 3, wy, wz), (12, cx + 1, cy, cz), (12, cx + 3, wy, wz),
            (3, cx + 1, cy, cz), (12, cx + 1, cy, cz), (2, cx + 2, cy, cz),
            (n, 1, 128), (n, 1, 128), (n - 1, 1, 128),
            (cy, 128), (cy, 128), (3, cy, 128), (3, cy, 128),
            (11, cx, cz), (LOW, cx, cz), (LOW, cx, cz), (11, cx, cz),
        ]
        adjoint, gradient = pl.pallas_call(
            functools.partial(kernel, sizes),
            out_shape=(jax.ShapeDtypeStruct(adjoint_load.shape, F32), jax.ShapeDtypeStruct((1, per), F32)),
            in_specs=[pl.BlockSpec(memory_space=pltpu.HBM)] * 6,
            out_specs=(vm, vm),
            scratch_shapes=[
                pltpu.VMEM(displacement.shape, F32), pltpu.VMEM(adjoint_load.shape, F32),
                pltpu.VMEM(bone_mask.shape, jnp.int32), pltpu.VMEM(elem_zone.shape, jnp.int32),
                pltpu.VMEM((rows, 128), jnp.int32), pltpu.SMEM((per,), F32)]
            + [pltpu.VMEM(s, F32) for s in scratch]
            + [pltpu.SemaphoreType.DMA] * 4 + [pltpu.SemaphoreType.DMA((10,))] * 2 + [pltpu.SemaphoreType.DMA((6,))],
            compiler_params=pltpu.CompilerParams(collective_id=0, has_side_effects=True, vmem_limit_bytes=40 * 2**20),
            cost_estimate=pl.CostEstimate(flops=10**7, bytes_accessed=10**6, transcendentals=0),
        )(*[pltpu.with_memory_space_constraint(v, pltpu.HBM) for v in (
            displacement, adjoint_load, bone_mask, elem_zone, zone_slot.reshape(-1, 128), zone_modulus)])
        return adjoint, gradient.reshape(per)

    whole = P(None, "gx", "gy", "gz")
    brick = P("gx", "gy", "gz")
    owned = P(("gx", "gy", "gz"))
    return jax.shard_map(on_device, mesh=mesh, in_specs=(whole, whole, brick, brick, P(), owned),
                         out_specs=(whole, owned), check_vma=False)
```

```python
import functools
import jax
import jax.numpy as jnp
from jax import lax
from jax.experimental import pallas as pl
from jax.experimental.pallas import tpu as pltpu
from jax.sharding import PartitionSpec as P

ZS = 16
SPRING = 0.1
MESH = pl.DeviceIdType.MESH
LAME = 0.3 / (1.3 * 0.4)
SHEAR = 0.5 / 1.3
F32 = jnp.float32
LOW = 5


def element_forces(m):
    c = 1.0 / 16.0
    lam, mu = c * LAME, c * SHEAR
    lam3, mu3 = lam / 3.0, mu / 3.0
    u, v, w = m
    f = [[[[None, None], [None, None]], [[None, None], [None, None]]] for _ in range(3)]
    div = lam * (u[1][0][0] + v[0][1][0] + w[0][0][1])
    f[0][1][0][0] = div + (2 * mu) * u[1][0][0]
    f[1][0][1][0] = div + (2 * mu) * v[0][1][0]
    f[2][0][0][1] = div + (2 * mu) * w[0][0][1]
    f[0][0][1][0] = f[1][1][0][0] = mu * (u[0][1][0] + v[1][0][0])
    f[1][0][0][1] = f[2][0][1][0] = mu * (v[0][0][1] + w[0][1][0])
    f[0][0][0][1] = f[2][1][0][0] = mu * (u[0][0][1] + w[1][0][0])
    t = lam3 * (u[1][1][0] + w[0][1][1])
    f[0][1][1][0] = t + mu * u[1][1][0]
    f[2][0][1][1] = t + mu * w[0][1][1]
    t = lam3 * (u[1][0][1] + v[0][1][1])
    f[0][1][0][1] = t + mu * u[1][0][1]
    f[1][0][1][1] = t + mu * v[0][1][1]
    t = lam3 * (v[1][1][0] + w[1][0][1])
    f[1][1][1][0] = t + mu * v[1][1][0]
    f[2][1][0][1] = t + mu * w[1][0][1]
    t = u[0][1][1] + v[1][0][1] + w[1][1][0]
    f[0][0][1][1] = mu3 * (t + u[0][1][1])
    f[1][1][0][1] = mu3 * (t + v[1][0][1])
    f[2][1][1][0] = mu3 * (t + w[1][1][0])
    for k in range(3):
        f[k][1][1][1] = ((lam + 4 * mu) / 9.0) * m[k][1][1][1]
    return f


def modes_of(load, x):
    out = []
    for k in range(3):
        here = [[load(4 * k + 2 * b + c, x) for c in range(2)] for b in range(2)]
        there = [[load(4 * k + 2 * b + c, x + 1) for c in range(2)] for b in range(2)]
        out.append([
            [[None if b + c == 0 else there[b][c] + here[b][c] for c in range(2)] for b in range(2)],
            [[there[b][c] - here[b][c] for c in range(2)] for b in range(2)],
        ])
    return out


ALL = [(k, a, b, c) for k in range(3) for a in range(2) for b in range(2) for c in range(2) if a + b + c]


def dot_modes(f, g):
    total = None
    for k, a, b, c in ALL:
        t = f[k][a][b][c] * g[k][a][b][c]
        total = t if total is None else total + t
    return total


def kernel(sizes, disp_in, load_in, mask_in, zone_in, slot_in, mod_in, adj_ref, grad_ref,
           disp, load, mask, zone, slot_ref, mod_ref,
           E, BM, DM, NB, Q, QM, TB, G, MS, R, ZPL, ZPH, ZL, ZH, YPL, YPH, YL, YH,
           ag_send, ag_recv, rs_send, rs_recv, hs, hr, ins):
    nx, ny, nz = sizes
    n = nx * ny * nz
    cx, cy, cz = mask.shape
    wy, wz = cy + 8, 2 * cz
    per = mod_ref.shape[0]
    rows = slot_ref.shape[0]
    ix, iy, iz = lax.axis_index("gx"), lax.axis_index("gy"), lax.axis_index("gz")
    me = (ix * ny + iy) * nz + iz

    barrier = pltpu.get_barrier_semaphore()
    offsets = [(a, b, c) for a in range(nx) for b in range(ny) for c in range(nz)][1:]

    def around(spot, step, count):
        if step == 0:
            return spot
        there = spot + step
        return jnp.where(there >= count, there - count, there)
    xs = [around(ix, a, nx) for a in range(nx)]
    ys = [around(iy, b, ny) for b in range(ny)]
    zs = [around(iz, c, nz) for c in range(nz)]

    def slot_at(a, b, c):
        return ((-a % nx) * ny + (-b % ny)) * nz + (-c % nz) - 1

    for a, b, c in offsets:
        pl.semaphore_signal(barrier, inc=1, device_id=(xs[a], ys[b], zs[c]), device_id_type=MESH)
    copies = [pltpu.make_async_copy(src, dst, ins.at[i]) for i, (src, dst) in enumerate(
        ((mod_in, mod_ref), (load_in, load), (mask_in, mask), (zone_in, zone), (disp_in, disp),
         (slot_in, slot_ref)))]
    for copy in copies:
        copy.start()
    for copy in copies:
        copy.wait()

    lane1 = lax.broadcasted_iota(jnp.int32, (1, 128), 1)
    row = jnp.zeros((1, 128), F32)
    for j in range(per):
        row = jnp.where(lane1 == (me * per) % 128 + j, mod_ref[j], row)
    G[me] = row

    def remote(src, dst, send, recv, device):
        return pltpu.make_async_remote_copy(
            src_ref=src, dst_ref=dst, send_sem=hs.at[send], recv_sem=hr.at[recv],
            device_id=device, device_id_type=MESH)

    def links(entries):
        for out, target, dst, _, source in entries:
            pl.when(target)(out.start)

            @pl.when(jnp.logical_not(source))
            def _(dst=dst):
                dst[...] = jnp.zeros(dst.shape, F32)

        def finish():
            for out, target, dst, sem, source in entries:
                pl.when(target)(out.wait_send)
                pl.when(source)(pltpu.make_async_copy(dst, dst, hr.at[sem]).wait)
        return finish

    def has(spot, step, count):
        return jnp.logical_and(spot + step >= 0, spot + step < count)

    def near(spot, step, count):
        return jnp.clip(spot + step, 0, count - 1)

    lane = lax.broadcasted_iota(jnp.int32, (cy, 128), 1)

    def fill(x, carry):
        low, high = carry
        for f in range(8):
            if f < 3:
                value = load[f, x]
            elif f == 3:
                value = mask[x].astype(F32)
            elif f == 4:
                value = zone[x].astype(F32)
            else:
                value = disp[f - 5, x]
            E[f, x + 1, 0:cy, 0:cz] = value
            low = jnp.where(lane == f * 8 + x, pltpu.roll(value, f * 8 + x, 1), low)
            if f < 3:
                low = jnp.where(lane == (8 + f) * 8 + x, pltpu.roll(value, (8 + f) * 8 + x - 1, 1), low)
            if f < LOW:
                high = jnp.where(lane == f * 8 + x, pltpu.roll(value, f * 8 + x + 1, 1), high)
        return low, high
    zero = jnp.zeros((cy, 128), F32)
    low, high = lax.fori_loop(0, cx, fill, (zero, zero), unroll=True)
    ZPL[...] = low
    ZPH[...] = high
    for f in range(8):
        YPL[f] = E[f, 1:cx + 1, 0, 0:cz]
        if f < 3:
            YPL[8 + f] = E[f, 1:cx + 1, 1, 0:cz]
        if f < LOW:
            YPH[f] = E[f, 1:cx + 1, cy - 1, 0:cz]
    pl.semaphore_wait(barrier, n - 1)
    entries = []
    for d in (0, -1, 1):
        for side, src, dst, step in ((0, ZPL, ZH, -1), (1, ZPH, ZL, 1)):
            target = jnp.logical_and(has(iy, d, ny), has(iz, step, nz))
            source = jnp.logical_and(has(iy, d, ny), has(iz, -step, nz))
            out = remote(src, dst.at[1 - d], 3 * side + 1 + d, 3 * side + 1 - d,
                         {"gy": near(iy, d, ny), "gz": near(iz, step, nz)})
            entries.append((out, target, dst.at[1 + d], 3 * side + 1 + d, source))
    for s, src, dst, step in ((6, YPL, YH, -1), (7, YPH, YL, 1)):
        out = remote(src, dst, s, s, {"gy": near(iy, step, ny)})
        entries.append((out, has(iy, step, ny), dst, s, has(iy, -step, ny)))
    finish_zy = links(entries)
    for a, b, c in offsets:
        pltpu.make_async_remote_copy(
            src_ref=G.at[me], dst_ref=G.at[me], send_sem=ag_send, recv_sem=ag_recv,
            device_id=(xs[a], ys[b], zs[c]), device_id_type=MESH).start()
    for i in range(12):
        NB[i, 1] = jnp.zeros((wy, wz), F32)
    finish_zy()

    line = lax.broadcasted_iota(jnp.int32, (8, 128), 0)
    tall = lax.broadcasted_iota(jnp.int32, (wy, 128), 1)

    def corners(ref):
        return jnp.concatenate([ref[1], jnp.where(
            line == 7, ref[0, cy - 8:cy], jnp.where(line < 2, ref[2, 0:8], 0.0))], axis=0)
    above_z, below_z = corners(ZH), corners(ZL)

    def open_z(x, carry):
        above, below = carry
        for f in range(8):
            tile = jnp.where(tall == 0, pltpu.roll(above, 128 - f * 8 - x, 1), 0.0)
            if f < 3:
                tile = jnp.where(tall == 1, pltpu.roll(above, 128 + 1 - (8 + f) * 8 - x, 1), tile)
            if f < LOW:
                tile = jnp.where(tall == 127, pltpu.roll(below, 127 - f * 8 - x, 1), tile)
            E[f, x + 1, :, cz:wz] = tile
        return carry
    lax.fori_loop(0, cx, open_z, (above_z, below_z), unroll=True)
    for f in range(8):
        above = YH[f]
        second = YH[8 + f] if f < 3 else None
        below = YL[f] if f < LOW else None
        for x in range(cx):
            tile = jnp.where(line == 0, above[x:x + 1], 0.0)
            if f < 3:
                tile = jnp.where(line == 1, second[x:x + 1], tile)
            if f < LOW:
                tile = jnp.where(line == 7, below[x:x + 1], tile)
            E[f, x + 1, cy:wy, 0:cz] = tile
    finish_x = links([
        (remote(E.at[:, pl.ds(1, 2)], E.at[:, pl.ds(cx + 1, 2)], 8, 8, {"gx": near(ix, -1, nx)}),
         has(ix, -1, nx), E.at[:, pl.ds(cx + 1, 2)], 8, has(ix, 1, nx)),
        (remote(E.at[pl.ds(0, LOW), pl.ds(cx, 1)], E.at[pl.ds(0, LOW), pl.ds(0, 1)], 9, 9,
                {"gx": near(ix, 1, nx)}),
         has(ix, 1, nx), E.at[pl.ds(0, LOW), pl.ds(0, 1)], 9, has(ix, -1, nx)),
    ])

    def yz_modes(v, put, x, k):
        after = pltpu.roll(v, wz - 1, 1)
        for c, t in enumerate((v + after, after - v)):
            above = pltpu.roll(t, wy - 1, 0)
            put(4 * k + c, x, t + above)
            put(4 * k + 2 + c, x, above - t)

    def put_b(i, x, v):
        BM[i, x] = v

    def put_d(i, x, v):
        DM[i, x] = v[0:cy, 0:cz]

    def put_q(i, x, v):
        QM[i, x] = v[0:cy, 0:cz]

    def b_modes(x, carry):
        for k in range(3):
            yz_modes(E[k, x], put_b, x, k)
        return carry

    def d_modes(x, carry):
        for k in range(3):
            yz_modes(E[5 + k, x + 1], put_d, x, k)
        return carry

    lax.fori_loop(0, cx, d_modes, 0, unroll=True)
    lax.fori_loop(1, cx + 1, b_modes, 0, unroll=True)

    whole = G.at[pl.ds(0, n - 1)]
    pltpu.make_async_copy(whole, whole, ag_recv).wait()
    group = n // rows
    by_slot = [jnp.sum(G[g * group:(g + 1) * group, 0, :], axis=0, keepdims=True) for g in range(rows)]

    def look_up(tables, index):
        tables = [jnp.broadcast_to(t, (8, 128)) for t in tables]
        low_bits, which = index % 128, index // 128
        out = None
        for g, t in enumerate(tables):
            got = jnp.take_along_axis(t, low_bits, axis=1, mode="promise_in_bounds")
            out = got if out is None else jnp.where(which == g, got, out)
        return out
    by_zone = []
    for g in range(rows):
        index = jnp.broadcast_to(slot_ref[g:g + 1, :], (8, 128))
        by_zone.append(look_up(by_slot, index)[0:1])

    def first(x, carry, lowest=False):
        where = E[4, x].astype(jnp.int32)
        parts = []
        for y in range(0, wy, 8):
            parts.append(jnp.concatenate(
                [look_up(by_zone, where[y:y + 8, z:z + 128]) for z in range(0, wz, 128)], axis=1))
        stiff = jnp.where(E[3, x] > 0.5, jnp.concatenate(parts, axis=0), 0.0)
        TB[1, x] = stiff[0:cy, 0:cz]
        f = element_forces(modes_of(lambda i, p: BM[i, p], x))

        def terms():
            inner = [[[[None if t is None else t[0:cy, 0:cz] for t in b] for b in a] for a in k] for k in f]
            TB[0, x] = dot_modes(inner, modes_of(lambda i, p: DM[i, p], x - 1))
        if not lowest:
            pl.when(x <= cx)(terms)
        for k in range(3):
            for b in range(2):
                for c in range(2):
                    i = 4 * k + 2 * b + c
                    delta = f[k][1][b][c] * stiff
                    if b + c:
                        total = f[k][0][b][c] * stiff
                        now, later = total - delta, total + delta
                    else:
                        now, later = -delta, delta
                    if lowest:
                        NB[i, 1] = NB[i, 1] + later
                    else:
                        NB[i, x] = NB[i, x] + now
                        NB[i, x + 1] = later
        return carry
    lax.fori_loop(1, cx, first, 0)
    finish_x()
    b_modes(0, 0)
    lax.fori_loop(cx + 1, cx + 3, b_modes, 0)
    d_modes(cx, 0)
    lax.fori_loop(cx, cx + 2, first, 0)
    first(0, 0, lowest=True)

    at_y = lax.broadcasted_iota(jnp.int32, (wy, wz), 0)
    at_z = lax.broadcasted_iota(jnp.int32, (wy, wz), 1)
    last_x, last_y, last_z = ix == nx - 1, iy == ny - 1, iz == nz - 1
    keep_y = jnp.where(last_y, cy, wy)
    keep_z = jnp.where(last_z, cz, wz)
    inside = jnp.logical_and(at_y < keep_y, at_z < keep_z)

    def nodes(x, carry):
        bq, qq, bb = carry
        keep_x = jnp.where(last_x, cx, cx + 1)
        valid = jnp.logical_and(inside, jnp.broadcast_to(x, (wy, wz)) < keep_x)
        own = jnp.where(x < cx, 1.0, 0.0).astype(F32)
        for k in range(3):
            side = []
            for c in range(2):
                s, d = NB[4 * k + c, x + 1], NB[4 * k + 2 + c, x + 1]
                side.append((s - d) + pltpu.roll(s + d, 1, 0))
            q = (side[0] - side[1]) + pltpu.roll(side[0] + side[1], 1, 1)
            q = jnp.where(valid, q, 0.0)
            mine = q[0:cy, 0:cz]
            Q[k, x] = mine
            v = E[k, x + 1, 0:cy, 0:cz]
            bq = bq + own * (v * mine)
            qq = qq + own * (mine * mine)
            bb = bb + own * (v * v)
            yz_modes(q, put_q, x, k)
        return bq, qq, bb
    bq, qq, bb = lax.fori_loop(0, cx + 1, nodes, (zero, zero, zero), unroll=True)

    scale = -(ZS ** -1.5)
    first_zone = zone[0]

    def second(x, carry):
        energy, a1, a2, b1, b2 = carry
        m = modes_of(lambda i, p: QM[i, p], x)
        f = element_forces(m)
        energy = energy + TB[1, x + 1] * dot_modes(f, m)
        bone = scale * mask[x].astype(F32)
        t2 = bone * dot_modes(f, modes_of(lambda i, p: DM[i, p], x))
        t1 = bone * TB[0, x + 1]
        same = zone[x] == first_zone
        a1 = a1 + jnp.where(same, t1, 0.0)
        a2 = a2 + jnp.where(same, t2, 0.0)
        b1 = b1 + jnp.where(same, 0.0, t1)
        b2 = b2 + jnp.where(same, 0.0, t2)
        return energy, a1, a2, b1, b2
    energy, a1, a2, b1, b2 = lax.fori_loop(0, cx, second, (zero,) * 5, unroll=True)

    owner = lax.broadcasted_iota(jnp.int32, (n, 128), 0)
    sub = lax.broadcasted_iota(jnp.int32, (16, 128), 0)
    slots = [slot_ref[g:g + 1, :] for g in range(rows)]
    out = jnp.zeros((n, 16), F32)
    for zones, t1, t2 in ((first_zone, a1, a2), (zone[cx - 1], b1, b2)):
        same = zones == zones[0:1]
        for at, cond in ((0, same), (cy - 1, jnp.logical_not(same))):
            v1 = jnp.sum(jnp.where(cond, t1, 0.0), axis=0, keepdims=True)
            v2 = jnp.sum(jnp.where(cond, t2, 0.0), axis=0, keepdims=True)
            k = look_up(slots, jnp.broadcast_to(zones[at:at + 1], (8, 128)))[0:1]
            own_by, part = k // per, k % per
            w = jnp.where(owner == own_by, 1.0, 0.0).astype(F32)
            v = jnp.where(sub == part, v1, jnp.where(sub == part + per, v2, 0.0))
            out = out + lax.dot_general(w, v, (((1,), (1,)), ((), ())),
                                        precision=lax.Precision.HIGHEST, preferred_element_type=F32)
    lane16 = lax.broadcasted_iota(jnp.int32, (n, 16), 1)
    for j, value in enumerate((bb, bq, qq, energy)):
        value = jnp.sum(jnp.sum(value, axis=0, keepdims=True), axis=1, keepdims=True)
        out = jnp.where(lane16 == 2 * per + j, value, out)
    MS[...] = jnp.zeros_like(MS)
    MS[:, 0, 0:16] = out

    for a, b, c in offsets:
        there = (xs[a], ys[b], zs[c])
        t = (there[0] * ny + there[1]) * nz + there[2]
        pltpu.make_async_remote_copy(
            src_ref=MS.at[t], dst_ref=R.at[slot_at(a, b, c)], send_sem=rs_send, recv_sem=rs_recv,
            device_id=there, device_id_type=MESH).start()
    pltpu.make_async_copy(R, R, rs_recv).wait()
    row = jnp.sum(R[:, 0, :], axis=0, keepdims=True) + MS[me]

    def pick(j):
        return jnp.sum(jnp.where(lane1 == 2 * per + j, row, 0.0), axis=1, keepdims=True)
    bb, bq, qq, qkq = pick(0), pick(1), pick(2), pick(3)
    gram = bb * qq - bq * bq
    top = SPRING * gram + (bb * qkq - bq * qq)
    det = SPRING * top + (bq * qkq - qq * qq)
    plane = det != 0.0
    c1 = jnp.where(plane, top / det, bb / (SPRING * bb + bq))
    c2 = jnp.where(plane, -gram / det, 0.0)
    both = c1 * row + c2 * pltpu.roll(row, 128 - per, 1)
    grad_ref[...] = both[:, 0:per]

    def finish(x, carry):
        for k in range(3):
            adj_ref[k, x] = c1 * load[k, x] + c2 * Q[k, x]
        return carry
    lax.fori_loop(0, cx, finish, 0, unroll=True)
    pltpu.make_async_copy(whole, whole, ag_send).wait()
    pltpu.make_async_copy(R, R, rs_send).wait()


def solution(mesh):
    sizes = (mesh.shape["gx"], mesh.shape["gy"], mesh.shape["gz"])
    n = sizes[0] * sizes[1] * sizes[2]

    def on_device(displacement, adjoint_load, bone_mask, elem_zone, zone_slot, zone_modulus):
        cx, cy, cz = bone_mask.shape
        per = zone_modulus.shape[0]
        wy, wz = cy + 8, 2 * cz
        vm = pl.BlockSpec(memory_space=pltpu.VMEM)
        rows = zone_slot.shape[0] // 128
        scratch = [
            (8, cx + 3, wy, wz), (12, cx + 3, wy, wz), (12, cx + 1, cy, cz), (12, cx + 3, wy, wz),
            (3, cx + 1, cy, cz), (12, cx + 1, cy, cz), (2, cx + 2, cy, cz),
            (n, 1, 128), (n, 1, 128), (n - 1, 1, 128),
            (cy, 128), (cy, 128), (3, cy, 128), (3, cy, 128),
            (11, cx, cz), (LOW, cx, cz), (LOW, cx, cz), (11, cx, cz),
        ]
        adjoint, gradient = pl.pallas_call(
            functools.partial(kernel, sizes),
            out_shape=(jax.ShapeDtypeStruct(adjoint_load.shape, F32), jax.ShapeDtypeStruct((1, per), F32)),
            in_specs=[pl.BlockSpec(memory_space=pltpu.HBM)] * 6,
            out_specs=(vm, vm),
            scratch_shapes=[
                pltpu.VMEM(displacement.shape, F32), pltpu.VMEM(adjoint_load.shape, F32),
                pltpu.VMEM(bone_mask.shape, jnp.int32), pltpu.VMEM(elem_zone.shape, jnp.int32),
                pltpu.VMEM((rows, 128), jnp.int32), pltpu.SMEM((per,), F32)]
            + [pltpu.VMEM(s, F32) for s in scratch]
            + [pltpu.SemaphoreType.DMA] * 4 + [pltpu.SemaphoreType.DMA((10,))] * 2 + [pltpu.SemaphoreType.DMA((6,))],
            compiler_params=pltpu.CompilerParams(collective_id=0, has_side_effects=True, vmem_limit_bytes=40 * 2**20),
            cost_estimate=pl.CostEstimate(flops=10**7, bytes_accessed=10**6, transcendentals=0),
        )(*[pltpu.with_memory_space_constraint(v, pltpu.HBM) for v in (
            displacement, adjoint_load, bone_mask, elem_zone, zone_slot.reshape(-1, 128), zone_modulus)])
        return adjoint, gradient.reshape(per)

    whole = P(None, "gx", "gy", "gz")
    brick = P("gx", "gy", "gz")
    owned = P(("gx", "gy", "gz"))
    return jax.shard_map(on_device, mesh=mesh, in_specs=(whole, whole, brick, brick, P(), owned),
                         out_specs=(whole, owned), check_vma=False)
```

```python
import functools
import jax
import jax.numpy as jnp
from jax import lax
from jax.experimental import pallas as pl
from jax.experimental.pallas import tpu as pltpu
from jax.sharding import PartitionSpec as P

ZS = 16
SPRING = 0.1
MESH = pl.DeviceIdType.MESH
LAME = 0.3 / (1.3 * 0.4)
SHEAR = 0.5 / 1.3
F32 = jnp.float32
LOW = 5


def element_forces(m):
    c = 1.0 / 16.0
    lam, mu = c * LAME, c * SHEAR
    lam3, mu3 = lam / 3.0, mu / 3.0
    u, v, w = m
    f = [[[[None, None], [None, None]], [[None, None], [None, None]]] for _ in range(3)]
    div = lam * (u[1][0][0] + v[0][1][0] + w[0][0][1])
    f[0][1][0][0] = div + (2 * mu) * u[1][0][0]
    f[1][0][1][0] = div + (2 * mu) * v[0][1][0]
    f[2][0][0][1] = div + (2 * mu) * w[0][0][1]
    f[0][0][1][0] = f[1][1][0][0] = mu * (u[0][1][0] + v[1][0][0])
    f[1][0][0][1] = f[2][0][1][0] = mu * (v[0][0][1] + w[0][1][0])
    f[0][0][0][1] = f[2][1][0][0] = mu * (u[0][0][1] + w[1][0][0])
    t = lam3 * (u[1][1][0] + w[0][1][1])
    f[0][1][1][0] = t + mu * u[1][1][0]
    f[2][0][1][1] = t + mu * w[0][1][1]
    t = lam3 * (u[1][0][1] + v[0][1][1])
    f[0][1][0][1] = t + mu * u[1][0][1]
    f[1][0][1][1] = t + mu * v[0][1][1]
    t = lam3 * (v[1][1][0] + w[1][0][1])
    f[1][1][1][0] = t + mu * v[1][1][0]
    f[2][1][0][1] = t + mu * w[1][0][1]
    t = u[0][1][1] + v[1][0][1] + w[1][1][0]
    f[0][0][1][1] = mu3 * (t + u[0][1][1])
    f[1][1][0][1] = mu3 * (t + v[1][0][1])
    f[2][1][1][0] = mu3 * (t + w[1][1][0])
    for k in range(3):
        f[k][1][1][1] = ((lam + 4 * mu) / 9.0) * m[k][1][1][1]
    return f


def modes_of(load, x):
    out = []
    for k in range(3):
        here = [[load(4 * k + 2 * b + c, x) for c in range(2)] for b in range(2)]
        there = [[load(4 * k + 2 * b + c, x + 1) for c in range(2)] for b in range(2)]
        out.append([
            [[None if b + c == 0 else there[b][c] + here[b][c] for c in range(2)] for b in range(2)],
            [[there[b][c] - here[b][c] for c in range(2)] for b in range(2)],
        ])
    return out


ALL = [(k, a, b, c) for k in range(3) for a in range(2) for b in range(2) for c in range(2) if a + b + c]


def dot_modes(f, g):
    total = None
    for k, a, b, c in ALL:
        t = f[k][a][b][c] * g[k][a][b][c]
        total = t if total is None else total + t
    return total


def kernel(sizes, disp_in, load_in, mask_in, zone_in, slot_in, mod_in, adj_ref, grad_ref,
           disp, load, mask, zone, slot_ref, mod_ref,
           E, BM, DM, NB, Q, QM, TB, G, MS, R, ZPL, ZPH, ZL, ZH, YPL, YPH, YL, YH,
           ag_send, ag_recv, rs_send, rs_recv, hs, hr, ins):
    nx, ny, nz = sizes
    n = nx * ny * nz
    cx, cy, cz = mask.shape
    wy, wz = cy + 8, 2 * cz
    per = mod_ref.shape[0]
    rows = slot_ref.shape[0]
    ix, iy, iz = lax.axis_index("gx"), lax.axis_index("gy"), lax.axis_index("gz")
    me = (ix * ny + iy) * nz + iz

    barrier = pltpu.get_barrier_semaphore()
    offsets = [(a, b, c) for a in range(nx) for b in range(ny) for c in range(nz)][1:]

    def around(spot, step, count):
        if step == 0:
            return spot
        there = spot + step
        return jnp.where(there >= count, there - count, there)
    xs = [around(ix, a, nx) for a in range(nx)]
    ys = [around(iy, b, ny) for b in range(ny)]
    zs = [around(iz, c, nz) for c in range(nz)]

    def slot_at(a, b, c):
        return ((-a % nx) * ny + (-b % ny)) * nz + (-c % nz) - 1

    for a, b, c in offsets:
        pl.semaphore_signal(barrier, inc=1, device_id=(xs[a], ys[b], zs[c]), device_id_type=MESH)
    copies = [pltpu.make_async_copy(src, dst, ins.at[i]) for i, (src, dst) in enumerate(
        ((mod_in, mod_ref), (load_in, load), (mask_in, mask), (zone_in, zone), (disp_in, disp),
         (slot_in, slot_ref)))]
    for copy in copies:
        copy.start()
    for copy in copies:
        copy.wait()

    lane1 = lax.broadcasted_iota(jnp.int32, (1, 128), 1)
    row = jnp.zeros((1, 128), F32)
    for j in range(per):
        row = jnp.where(lane1 == (me * per) % 128 + j, mod_ref[j], row)
    G[me] = row

    def remote(src, dst, send, recv, device):
        return pltpu.make_async_remote_copy(
            src_ref=src, dst_ref=dst, send_sem=hs.at[send], recv_sem=hr.at[recv],
            device_id=device, device_id_type=MESH)

    def links(entries):
        for out, target, dst, _, source in entries:
            pl.when(target)(out.start)

            @pl.when(jnp.logical_not(source))
            def _(dst=dst):
                dst[...] = jnp.zeros(dst.shape, F32)

        def finish():
            for out, target, dst, sem, source in entries:
                pl.when(target)(out.wait_send)
                pl.when(source)(pltpu.make_async_copy(dst, dst, hr.at[sem]).wait)
        return finish

    def has(spot, step, count):
        return jnp.logical_and(spot + step >= 0, spot + step < count)

    def near(spot, step, count):
        return jnp.clip(spot + step, 0, count - 1)

    lane = lax.broadcasted_iota(jnp.int32, (cy, 128), 1)

    def fill(x, carry):
        low, high = carry
        for f in range(8):
            if f < 3:
                value = load[f, x]
            elif f == 3:
                value = mask[x].astype(F32)
            elif f == 4:
                value = zone[x].astype(F32)
            else:
                value = disp[f - 5, x]
            E[f, x + 1, 0:cy, 0:cz] = value
            low = jnp.where(lane == f * 8 + x, pltpu.roll(value, f * 8 + x, 1), low)
            if f < 3:
                low = jnp.where(lane == (8 + f) * 8 + x, pltpu.roll(value, (8 + f) * 8 + x - 1, 1), low)
            if f < LOW:
                high = jnp.where(lane == f * 8 + x, pltpu.roll(value, f * 8 + x + 1, 1), high)
        return low, high
    zero = jnp.zeros((cy, 128), F32)
    low, high = lax.fori_loop(0, cx, fill, (zero, zero), unroll=True)
    ZPL[...] = low
    ZPH[...] = high
    for f in range(8):
        YPL[f] = E[f, 1:cx + 1, 0, 0:cz]
        if f < 3:
            YPL[8 + f] = E[f, 1:cx + 1, 1, 0:cz]
        if f < LOW:
            YPH[f] = E[f, 1:cx + 1, cy - 1, 0:cz]
    pl.semaphore_wait(barrier, n - 1)
    entries = []
    for d in (0, -1, 1):
        for side, src, dst, step in ((0, ZPL, ZH, -1), (1, ZPH, ZL, 1)):
            target = jnp.logical_and(has(iy, d, ny), has(iz, step, nz))
            source = jnp.logical_and(has(iy, d, ny), has(iz, -step, nz))
            out = remote(src, dst.at[1 - d], 3 * side + 1 + d, 3 * side + 1 - d,
                         {"gy": near(iy, d, ny), "gz": near(iz, step, nz)})
            entries.append((out, target, dst.at[1 + d], 3 * side + 1 + d, source))
    for s, src, dst, step in ((6, YPL, YH, -1), (7, YPH, YL, 1)):
        out = remote(src, dst, s, s, {"gy": near(iy, step, ny)})
        entries.append((out, has(iy, step, ny), dst, s, has(iy, -step, ny)))
    finish_zy = links(entries)
    for a, b, c in offsets:
        pltpu.make_async_remote_copy(
            src_ref=G.at[me], dst_ref=G.at[me], send_sem=ag_send, recv_sem=ag_recv,
            device_id=(xs[a], ys[b], zs[c]), device_id_type=MESH).start()
    for i in range(12):
        NB[i, 1] = jnp.zeros((wy, wz), F32)
    finish_zy()

    line = lax.broadcasted_iota(jnp.int32, (8, 128), 0)
    tall = lax.broadcasted_iota(jnp.int32, (wy, 128), 1)

    def corners(ref):
        return jnp.concatenate([ref[1], jnp.where(
            line == 7, ref[0, cy - 8:cy], jnp.where(line < 2, ref[2, 0:8], 0.0))], axis=0)
    above_z, below_z = corners(ZH), corners(ZL)

    def open_z(x, carry):
        above, below = carry
        for f in range(8):
            tile = jnp.where(tall == 0, pltpu.roll(above, 128 - f * 8 - x, 1), 0.0)
            if f < 3:
                tile = jnp.where(tall == 1, pltpu.roll(above, 128 + 1 - (8 + f) * 8 - x, 1), tile)
            if f < LOW:
                tile = jnp.where(tall == 127, pltpu.roll(below, 127 - f * 8 - x, 1), tile)
            E[f, x + 1, :, cz:wz] = tile
        return carry
    lax.fori_loop(0, cx, open_z, (above_z, below_z), unroll=True)
    for f in range(8):
        above = YH[f]
        second = YH[8 + f] if f < 3 else None
        below = YL[f] if f < LOW else None
        for x in range(cx):
            tile = jnp.where(line == 0, above[x:x + 1], 0.0)
            if f < 3:
                tile = jnp.where(line == 1, second[x:x + 1], tile)
            if f < LOW:
                tile = jnp.where(line == 7, below[x:x + 1], tile)
            E[f, x + 1, cy:wy, 0:cz] = tile
    finish_x = links([
        (remote(E.at[:, pl.ds(1, 2)], E.at[:, pl.ds(cx + 1, 2)], 8, 8, {"gx": near(ix, -1, nx)}),
         has(ix, -1, nx), E.at[:, pl.ds(cx + 1, 2)], 8, has(ix, 1, nx)),
        (remote(E.at[pl.ds(0, LOW), pl.ds(cx, 1)], E.at[pl.ds(0, LOW), pl.ds(0, 1)], 9, 9,
                {"gx": near(ix, 1, nx)}),
         has(ix, 1, nx), E.at[pl.ds(0, LOW), pl.ds(0, 1)], 9, has(ix, -1, nx)),
    ])

    def yz_modes(v, put, x, k):
        after = pltpu.roll(v, wz - 1, 1)
        for c, t in enumerate((v + after, after - v)):
            above = pltpu.roll(t, wy - 1, 0)
            put(4 * k + c, x, t + above)
            put(4 * k + 2 + c, x, above - t)

    def put_b(i, x, v):
        BM[i, x] = v

    def put_d(i, x, v):
        DM[i, x] = v[0:cy, 0:cz]

    def put_q(i, x, v):
        QM[i, x] = v[0:cy, 0:cz]

    def b_modes(x, carry):
        for k in range(3):
            yz_modes(E[k, x], put_b, x, k)
        return carry

    def d_modes(x, carry):
        for k in range(3):
            yz_modes(E[5 + k, x + 1], put_d, x, k)
        return carry

    lax.fori_loop(0, cx, d_modes, 0, unroll=True)
    lax.fori_loop(1, cx + 1, b_modes, 0, unroll=True)

    whole = G.at[pl.ds(0, n - 1)]
    pltpu.make_async_copy(whole, whole, ag_recv).wait()
    group = n // rows
    by_slot = [jnp.sum(G[g * group:(g + 1) * group, 0, :], axis=0, keepdims=True) for g in range(rows)]

    def look_up(tables, index):
        tables = [jnp.broadcast_to(t, (8, 128)) for t in tables]
        low_bits, which = index % 128, index // 128
        out = None
        for g, t in enumerate(tables):
            got = jnp.take_along_axis(t, low_bits, axis=1, mode="promise_in_bounds")
            out = got if out is None else jnp.where(which == g, got, out)
        return out
    by_zone = []
    for g in range(rows):
        index = jnp.broadcast_to(slot_ref[g:g + 1, :], (8, 128))
        by_zone.append(look_up(by_slot, index)[0:1])

    def first(x, carry, lowest=False):
        where = E[4, x].astype(jnp.int32)
        parts = []
        for y in range(0, wy, 8):
            parts.append(jnp.concatenate(
                [look_up(by_zone, where[y:y + 8, z:z + 128]) for z in range(0, wz, 128)], axis=1))
        stiff = jnp.where(E[3, x] > 0.5, jnp.concatenate(parts, axis=0), 0.0)
        TB[1, x] = stiff[0:cy, 0:cz]
        f = element_forces(modes_of(lambda i, p: BM[i, p], x))

        def terms():
            inner = [[[[None if t is None else t[0:cy, 0:cz] for t in b] for b in a] for a in k] for k in f]
            TB[0, x] = dot_modes(inner, modes_of(lambda i, p: DM[i, p], x - 1))
        if not lowest:
            pl.when(x <= cx)(terms)
        for k in range(3):
            for b in range(2):
                for c in range(2):
                    i = 4 * k + 2 * b + c
                    delta = f[k][1][b][c] * stiff
                    if b + c:
                        total = f[k][0][b][c] * stiff
                        now, later = total - delta, total + delta
                    else:
                        now, later = -delta, delta
                    if lowest:
                        NB[i, 1] = NB[i, 1] + later
                    else:
                        NB[i, x] = NB[i, x] + now
                        NB[i, x + 1] = later
        return carry
    lax.fori_loop(1, cx, first, 0, unroll=True)
    finish_x()
    b_modes(0, 0)
    lax.fori_loop(cx + 1, cx + 3, b_modes, 0, unroll=True)
    d_modes(cx, 0)
    lax.fori_loop(cx, cx + 2, first, 0, unroll=True)
    first(0, 0, lowest=True)

    at_y = lax.broadcasted_iota(jnp.int32, (wy, wz), 0)
    at_z = lax.broadcasted_iota(jnp.int32, (wy, wz), 1)
    last_x, last_y, last_z = ix == nx - 1, iy == ny - 1, iz == nz - 1
    keep_y = jnp.where(last_y, cy, wy)
    keep_z = jnp.where(last_z, cz, wz)
    inside = jnp.logical_and(at_y < keep_y, at_z < keep_z)

    def nodes(x, carry):
        bq, qq, bb = carry
        keep_x = jnp.where(last_x, cx, cx + 1)
        valid = jnp.logical_and(inside, jnp.broadcast_to(x, (wy, wz)) < keep_x)
        own = jnp.where(x < cx, 1.0, 0.0).astype(F32)
        for k in range(3):
            side = []
            for c in range(2):
                s, d = NB[4 * k + c, x + 1], NB[4 * k + 2 + c, x + 1]
                side.append((s - d) + pltpu.roll(s + d, 1, 0))
            q = (side[0] - side[1]) + pltpu.roll(side[0] + side[1], 1, 1)
            q = jnp.where(valid, q, 0.0)
            mine = q[0:cy, 0:cz]
            Q[k, x] = mine
            v = E[k, x + 1, 0:cy, 0:cz]
            bq = bq + own * (v * mine)
            qq = qq + own * (mine * mine)
            bb = bb + own * (v * v)
            yz_modes(q, put_q, x, k)
        return bq, qq, bb
    bq, qq, bb = lax.fori_loop(0, cx + 1, nodes, (zero, zero, zero), unroll=True)

    scale = -(ZS ** -1.5)
    first_zone = zone[0]

    def second(x, carry):
        energy, a1, a2, b1, b2 = carry
        m = modes_of(lambda i, p: QM[i, p], x)
        f = element_forces(m)
        energy = energy + TB[1, x + 1] * dot_modes(f, m)
        bone = scale * mask[x].astype(F32)
        t2 = bone * dot_modes(f, modes_of(lambda i, p: DM[i, p], x))
        t1 = bone * TB[0, x + 1]
        same = zone[x] == first_zone
        a1 = a1 + jnp.where(same, t1, 0.0)
        a2 = a2 + jnp.where(same, t2, 0.0)
        b1 = b1 + jnp.where(same, 0.0, t1)
        b2 = b2 + jnp.where(same, 0.0, t2)
        return energy, a1, a2, b1, b2
    energy, a1, a2, b1, b2 = lax.fori_loop(0, cx, second, (zero,) * 5, unroll=True)

    owner = lax.broadcasted_iota(jnp.int32, (n, 128), 0)
    sub = lax.broadcasted_iota(jnp.int32, (16, 128), 0)
    slots = [slot_ref[g:g + 1, :] for g in range(rows)]
    out = jnp.zeros((n, 16), F32)
    for zones, t1, t2 in ((first_zone, a1, a2), (zone[cx - 1], b1, b2)):
        same = zones == zones[0:1]
        for at, cond in ((0, same), (cy - 1, jnp.logical_not(same))):
            v1 = jnp.sum(jnp.where(cond, t1, 0.0), axis=0, keepdims=True)
            v2 = jnp.sum(jnp.where(cond, t2, 0.0), axis=0, keepdims=True)
            k = look_up(slots, jnp.broadcast_to(zones[at:at + 1], (8, 128)))[0:1]
            own_by, part = k // per, k % per
            w = jnp.where(owner == own_by, 1.0, 0.0).astype(F32)
            v = jnp.where(sub == part, v1, jnp.where(sub == part + per, v2, 0.0))
            out = out + lax.dot_general(w, v, (((1,), (1,)), ((), ())),
                                        precision=lax.Precision.HIGHEST, preferred_element_type=F32)
    lane16 = lax.broadcasted_iota(jnp.int32, (n, 16), 1)
    for j, value in enumerate((bb, bq, qq, energy)):
        value = jnp.sum(jnp.sum(value, axis=0, keepdims=True), axis=1, keepdims=True)
        out = jnp.where(lane16 == 2 * per + j, value, out)
    MS[...] = jnp.zeros_like(MS)
    MS[:, 0, 0:16] = out

    for a, b, c in offsets:
        there = (xs[a], ys[b], zs[c])
        t = (there[0] * ny + there[1]) * nz + there[2]
        pltpu.make_async_remote_copy(
            src_ref=MS.at[t], dst_ref=R.at[slot_at(a, b, c)], send_sem=rs_send, recv_sem=rs_recv,
            device_id=there, device_id_type=MESH).start()
    pltpu.make_async_copy(R, R, rs_recv).wait()
    row = jnp.sum(R[:, 0, :], axis=0, keepdims=True) + MS[me]

    def pick(j):
        return jnp.sum(jnp.where(lane1 == 2 * per + j, row, 0.0), axis=1, keepdims=True)
    bb, bq, qq, qkq = pick(0), pick(1), pick(2), pick(3)
    gram = bb * qq - bq * bq
    top = SPRING * gram + (bb * qkq - bq * qq)
    det = SPRING * top + (bq * qkq - qq * qq)
    plane = det != 0.0
    c1 = jnp.where(plane, top / det, bb / (SPRING * bb + bq))
    c2 = jnp.where(plane, -gram / det, 0.0)
    both = c1 * row + c2 * pltpu.roll(row, 128 - per, 1)
    grad_ref[...] = both[:, 0:per]

    def finish(x, carry):
        for k in range(3):
            adj_ref[k, x] = c1 * load[k, x] + c2 * Q[k, x]
        return carry
    lax.fori_loop(0, cx, finish, 0, unroll=True)
    pltpu.make_async_copy(whole, whole, ag_send).wait()
    pltpu.make_async_copy(R, R, rs_send).wait()


def solution(mesh):
    sizes = (mesh.shape["gx"], mesh.shape["gy"], mesh.shape["gz"])
    n = sizes[0] * sizes[1] * sizes[2]

    def on_device(displacement, adjoint_load, bone_mask, elem_zone, zone_slot, zone_modulus):
        cx, cy, cz = bone_mask.shape
        per = zone_modulus.shape[0]
        wy, wz = cy + 8, 2 * cz
        vm = pl.BlockSpec(memory_space=pltpu.VMEM)
        rows = zone_slot.shape[0] // 128
        scratch = [
            (8, cx + 3, wy, wz), (12, cx + 3, wy, wz), (12, cx + 1, cy, cz), (12, cx + 3, wy, wz),
            (3, cx + 1, cy, cz), (12, cx + 1, cy, cz), (2, cx + 2, cy, cz),
            (n, 1, 128), (n, 1, 128), (n - 1, 1, 128),
            (cy, 128), (cy, 128), (3, cy, 128), (3, cy, 128),
            (11, cx, cz), (LOW, cx, cz), (LOW, cx, cz), (11, cx, cz),
        ]
        adjoint, gradient = pl.pallas_call(
            functools.partial(kernel, sizes),
            out_shape=(jax.ShapeDtypeStruct(adjoint_load.shape, F32), jax.ShapeDtypeStruct((1, per), F32)),
            in_specs=[pl.BlockSpec(memory_space=pltpu.HBM)] * 6,
            out_specs=(vm, vm),
            scratch_shapes=[
                pltpu.VMEM(displacement.shape, F32), pltpu.VMEM(adjoint_load.shape, F32),
                pltpu.VMEM(bone_mask.shape, jnp.int32), pltpu.VMEM(elem_zone.shape, jnp.int32),
                pltpu.VMEM((rows, 128), jnp.int32), pltpu.SMEM((per,), F32)]
            + [pltpu.VMEM(s, F32) for s in scratch]
            + [pltpu.SemaphoreType.DMA] * 4 + [pltpu.SemaphoreType.DMA((10,))] * 2 + [pltpu.SemaphoreType.DMA((6,))],
            compiler_params=pltpu.CompilerParams(collective_id=0, has_side_effects=True, vmem_limit_bytes=40 * 2**20),
            cost_estimate=pl.CostEstimate(flops=10**7, bytes_accessed=10**6, transcendentals=0),
        )(*[pltpu.with_memory_space_constraint(v, pltpu.HBM) for v in (
            displacement, adjoint_load, bone_mask, elem_zone, zone_slot.reshape(-1, 128), zone_modulus)])
        return adjoint, gradient.reshape(per)

    whole = P(None, "gx", "gy", "gz")
    brick = P("gx", "gy", "gz")
    owned = P(("gx", "gy", "gz"))
    return jax.shard_map(on_device, mesh=mesh, in_specs=(whole, whole, brick, brick, P(), owned),
                         out_specs=(whole, owned), check_vma=False)
```
